32 devices in a mesh: groups: 2 (over y), ex: 16 (over z, x, core).
Axes of the slice: x: 2, y: 2, z: 4, core: 2. Of those that a mesh axis runs over, the one named last changes fastest.
Arguments:
- gradient_mantissas: bfloat16 [4096, 4096], P(('groups', 'ex')), parts along dimension 0, may hold values from -6 to 6
- gradient_exponents: int32 [4096, 32], P(('groups', 'ex')), parts along dimension 0, may hold values from -2 to 2
- routes: int32 [4096, 8], P(('groups', 'ex')), parts along dimension 0, may hold values from 0 to 15, all different within a row; in each aligned block of 128 rows (0 to 127, 128 to 255, ...) at most 80 rows name the same one
- routing_weight: bfloat16 [4096, 8], P(('groups', 'ex')), parts along dimension 0, may hold values from 0.019897461 to 0.5
- stored_hidden_rows: bfloat16 [32, 16, 80, 768], P(('groups', 'ex')), parts along dimension 0, may hold values from -0.29882812 to 0.29882812
- frozen_down_weight: bfloat16 [16, 768, 4096], P('ex'), may hold values from -0.21875 to 0.21875
- adapter_first_factor: bfloat16 [768, 32], replicated, may hold values from -0.21875 to 0.21875
- adapter_second_factor: bfloat16 [32, 4096], replicated, may hold values from -0.44921875 to 0.44921875
- expert_adapter_gate: float32 [16], replicated, may hold values from 0.25 to 1
Outputs:
- hidden_gradient: bfloat16 [32, 16, 80, 768], P(('groups', 'ex')), parts along dimension 0
- routing_gradient: float32 [4096, 8], P(('groups', 'ex')), parts along dimension 0
- first_factor_gradient: float32 [1536, 32], P('groups'), parts along dimension 0
- second_factor_gradient: float32 [64, 4096], P('groups'), parts along dimension 0
- gate_grad: float32 [32], P('groups'), parts along dimension 0
The draws below stay inside these ranges and needn't reach their ends.
There are 2 independent parts, one for each index of `groups`. The reference program is written for one: setup_inputs(seed, part) draws one part's arguments, and reference() takes and returns one part's arrays. A program takes and returns all parts, laid end to end along the dimension named above; an argument that names none is the same for every part. Nothing has to cross between parts.
Inputs may be any that keep to these rules, and one draw needn't show every extreme that they name: `routes`: each token names 8 different experts; the 128 tokens of one device name one expert at most 80 times.
All inputs are finite; a program needn't handle non-finite values.
Results may differ from the reference program's by a relative error of at most 0.0052.
Values may be sent and summed in bfloat16 or wider, within the bound.
No kernel may reach another device: no remote copies, remote signals or barrier semaphores. Data moves between devices by JAX's collectives and lax.ppermute only.
A program may use at most 128 MiB of HBM per device.

```python
import math
import jax
import jax.numpy as jnp
import numpy as np
from jax import lax

MODEL_WIDTH = 4096
HIDDEN_UNITS = 768
TOP = 8
ADAPTER_RANK = 32
SCALE_BLOCK = 128
TOK_DEV = 128
EXPERTS = 16
SOURCES = 16
TOKENS = 2048
CAP = 80


def touch_ends(drawn, rng, smallest, largest):
    extent = drawn.shape
    spot = [jax.random.randint(jax.random.fold_in(rng, axis), (), 0, extent[axis]) for axis in range(len(extent))]
    drawn = drawn.at[tuple(spot)].set(smallest)
    longest = extent.index(max(extent))
    spot[longest] = (spot[longest] + 1) % extent[longest]
    return drawn.at[tuple(spot)].set(largest)


def steps_of(key, dims, shards, low, top_value):
    def one(dim, blocks):
        draws = jax.random.uniform(jax.random.fold_in(jax.random.fold_in(key, 6), dim), (blocks,), jnp.float32, low / len(shards), top_value / len(shards))
        return jnp.repeat(jnp.exp(draws), dims[dim] // blocks).reshape((-1,) + (1,) * (len(dims) - dim - 1))

    level = one(*shards[0])
    for cut in shards[1:]:
        level = level * one(*cut)
    return level


def routed_block(rng, own, number, rows, amount, top, limit, lean):
    ranking = jax.random.permutation(rng, amount)
    packed, usual = load_shares(amount, rows * top, limit, lean, True), load_shares(amount, rows * top, limit, lean, False)
    places = jnp.arange(amount)

    def named(tallies, turn):
        used = int((tallies > 0).sum())
        fixed = max(1, used // 4)
        passed = fixed + (places - fixed + turn * (used - fixed)) % max(1, amount - fixed)
        return jnp.zeros((amount,), jnp.int32).at[ranking[jnp.where(places < fixed, places, passed)]].set(jnp.asarray(tallies, jnp.int32))

    tallies = jnp.where(number % 4 == 0, named(packed, number // 4), named(usual, number - number // 4 - 1))
    mixed = jax.random.permutation(jax.random.fold_in(own, 3), amount)
    giver, sink = mixed[0:amount // 2 * 2:2], mixed[1:amount // 2 * 2:2]
    room = jnp.minimum(tallies[giver] - 1, limit - tallies[sink]) // 2
    room = jnp.where((giver == ranking[0]) | (sink == ranking[0]) | (tallies[sink] == 0), 0, jnp.maximum(room, 0))
    passed = jax.random.randint(jax.random.fold_in(own, 4), (amount // 2,), 0, 1 << 20) % (room + 1)
    tallies = tallies.at[giver].add(-passed).at[sink].add(passed)
    labels = jnp.searchsorted(jnp.cumsum(tallies), jnp.arange(rows * top), side="right").astype(jnp.int32)
    listing = labels.reshape(top, rows).T
    listing = listing[jax.random.permutation(jax.random.fold_in(own, 1), rows)]
    turn = jax.random.randint(jax.random.fold_in(own, 2), (rows, 1), 0, top)
    return jnp.take_along_axis(listing, (jnp.arange(top)[None, :] + turn) % top, axis=1)


def load_shares(count, total, limit, skew, full):
    loads = [(1 << 20) // math.isqrt(grade ** skew) + 1 for grade in range(1, count + 1)]
    largest = limit if full else min(limit, max(-(-total // count), total * loads[0] // sum(loads)))
    least = 1 if total - largest >= count - 1 else 0
    holding, spare = [largest] + [least] * (count - 1), total - largest - least * (count - 1)
    while spare > 0:
        candidates = [i for i in range(1, count) if holding[i] < largest] or [i for i in range(1, count) if holding[i] < limit]
        whole, budget = sum([loads[i] for i in candidates]), spare
        for i in candidates:
            more = min(limit - holding[i], max(1, budget * loads[i] // whole), spare)
            holding[i] = holding[i] + more
            spare = spare - more
    return np.array(holding)


def centred(key, dims, spread, reach, shards=(), kind=jnp.bfloat16):
    loudness = steps_of(key, dims, shards, -0.22, 0.18) if shards else 1.0
    array = jax.random.normal(key, dims, jnp.float32) * spread * loudness
    return jnp.minimum(jnp.maximum(array, -reach), reach).astype(kind)


def setup_inputs(seed: int = 0, part: int = 0) -> dict:
    keys = jax.random.split(jax.random.key(seed), 10)
    part_keys = jax.random.split(jax.random.fold_in(keys[9], part), 10)
    gradient_mantissas = centred(part_keys[0], (TOKENS, MODEL_WIDTH), 1.0, 6.0, ((0, 16),))
    gradient_exponents = touch_ends(jax.random.randint(part_keys[1], (TOKENS, MODEL_WIDTH // SCALE_BLOCK), -2, 3), jax.random.fold_in(part_keys[1], 1), -2, 2).astype(jnp.int32)
    routes_keys = jax.random.split(jax.random.fold_in(part_keys[2], 1), TOKENS // TOK_DEV)
    routes_turns = jax.random.permutation(jax.random.fold_in(part_keys[2], 3), TOKENS // TOK_DEV)
    routes = jax.vmap(lambda own, number: routed_block(jax.random.fold_in(part_keys[2], 2), own, number, TOK_DEV, EXPERTS, TOP, CAP, 2))(routes_keys, routes_turns).reshape((TOKENS, TOP))
    routing_weight = jnp.clip(jnp.exp(math.log(0.5) - 3.224016 * jax.random.uniform(part_keys[3], (TOKENS, TOP), jnp.float32) ** steps_of(part_keys[3], (TOKENS, TOP), ((0, 16),), -0.2, 0.2)), 0.019897461, 0.5).astype(jnp.bfloat16)
    stored_hidden_rows = centred(part_keys[4], (EXPERTS, SOURCES, CAP, HIDDEN_UNITS), 0.04, 0.29882812, ((0, 16),))
    frozen_down_weight = centred(keys[5], (EXPERTS, HIDDEN_UNITS, MODEL_WIDTH), HIDDEN_UNITS ** -0.5, 0.21875, ((0, 16),))
    adapter_first_factor = centred(keys[6], (HIDDEN_UNITS, ADAPTER_RANK), HIDDEN_UNITS ** -0.5, 0.21875)
    adapter_second_factor = centred(keys[7], (ADAPTER_RANK, MODEL_WIDTH), 0.075, 0.44921875)
    expert_adapter_gate = jnp.clip(jnp.exp(jax.random.uniform(keys[8], (EXPERTS,), jnp.float32, math.log(0.25), math.log(1.0))), 0.25, 1.0)
    return {"gradient_mantissas": gradient_mantissas, "gradient_exponents": gradient_exponents, "routes": routes, "routing_weight": routing_weight, "stored_hidden_rows": stored_hidden_rows, "frozen_down_weight": frozen_down_weight, "adapter_first_factor": adapter_first_factor, "adapter_second_factor": adapter_second_factor, "expert_adapter_gate": expert_adapter_gate}


def block_scale(gradient_exponents):
    scaling = jnp.zeros(gradient_exponents.shape, jnp.float32)
    for exponent in range(-2, 3):
        scaling = scaling + jnp.where(gradient_exponents == exponent, jnp.float32(2.0 ** exponent), jnp.float32(0.0))
    return scaling

def expand_grad(gradient_mantissas, gradient_exponents):
    blocks = gradient_exponents.shape[1]
    scaling = block_scale(gradient_exponents)
    widened = gradient_mantissas.astype(jnp.float32).reshape(gradient_mantissas.shape[0], blocks, -1) * scaling[:, :, None]
    return widened.reshape(gradient_mantissas.shape).astype(jnp.bfloat16)

def slot_table(route_block, experts, capacity):
    flat_routes = route_block.reshape(-1).astype(jnp.int32)
    onehot = (flat_routes[:, None] == jnp.arange(experts, dtype=jnp.int32)[None, :]).astype(jnp.int32)
    running = (jnp.cumsum(onehot, axis=0) - 1).astype(jnp.int32)
    slot_index = lax.optimization_barrier(jnp.sum(running * onehot, axis=1)).astype(jnp.int32)
    return (flat_routes * capacity + slot_index).astype(jnp.int32)

def per_expert_terms(current_row_block, routing_share, reduced_input, stored_rows, expert_down_matrix, adapter_first_factor, expert_gate_value):
    contract_dimensions = (((1,), (1,)), ((), ()))
    base_term = lax.dot_general(current_row_block, expert_down_matrix, contract_dimensions, preferred_element_type=jnp.float32)
    adapter_side_term = lax.dot_general(reduced_input, adapter_first_factor, contract_dimensions, preferred_element_type=jnp.float32)
    combined = base_term + expert_gate_value * adapter_side_term
    share_col = routing_share.astype(jnp.float32)[:, None]
    hidden_gradient = (share_col * combined).astype(jnp.bfloat16)
    weight_grad = lax.optimization_barrier(jnp.sum(stored_rows.astype(jnp.float32) * combined, axis=1))
    low_float = reduced_input.astype(jnp.float32)
    rows_dims = (((0,), (0,)), ((), ()))
    pushed = (expert_gate_value * share_col * low_float).astype(jnp.bfloat16)
    a_grad = lax.dot_general(stored_rows, pushed, rows_dims, preferred_element_type=jnp.float32)
    reduced_rank_rows = jnp.dot(stored_rows, adapter_first_factor, preferred_element_type=jnp.float32)
    pulled = (expert_gate_value * share_col * reduced_rank_rows).astype(jnp.bfloat16)
    b_grad = lax.dot_general(pulled, current_row_block, rows_dims, preferred_element_type=jnp.float32)
    gate_term = jnp.sum(routing_share.astype(jnp.float32) * lax.optimization_barrier(jnp.sum(reduced_rank_rows * low_float, axis=1)))
    return (hidden_gradient, weight_grad, a_grad, b_grad, gate_term)

def reference(gradient_mantissas, gradient_exponents, routes, routing_weight, stored_hidden_rows, frozen_down_weight, adapter_first_factor, adapter_second_factor, expert_adapter_gate):
    grad_out = expand_grad(gradient_mantissas, gradient_exponents)
    route_blocks = routes.reshape(SOURCES, TOK_DEV, TOP)
    dest = jax.vmap(lambda block: slot_table(block, EXPERTS, CAP))(route_blocks)
    local_token = jnp.arange(TOK_DEV * TOP, dtype=jnp.int32) // TOP
    global_token = local_token[None, :] + (jnp.arange(SOURCES, dtype=jnp.int32) * TOK_DEV)[:, None]
    source_ids = jnp.broadcast_to(jnp.arange(SOURCES, dtype=jnp.int32)[:, None], dest.shape)
    token_of = jnp.zeros((SOURCES, EXPERTS * CAP), jnp.int32).at[source_ids, dest].set(global_token)
    filled = jnp.zeros((SOURCES, EXPERTS * CAP), jnp.int32).at[source_ids, dest].set(1)
    share_table = jnp.zeros((SOURCES, EXPERTS * CAP), jnp.bfloat16).at[source_ids, dest].set(routing_weight.reshape(SOURCES, -1))
    token_of = token_of.reshape(SOURCES, EXPERTS, CAP).transpose(1, 0, 2)
    filled = filled.reshape(SOURCES, EXPERTS, CAP).transpose(1, 0, 2)
    share_table = share_table.reshape(SOURCES, EXPERTS, CAP).transpose(1, 0, 2)

    def one_expert(expert_number):
        token_ids = token_of[expert_number].reshape(-1)
        occupied = filled[expert_number].reshape(-1)
        current_row_block = jnp.where(occupied[:, None] > 0, grad_out[token_ids], jnp.zeros((), jnp.bfloat16))
        routing_share = share_table[expert_number].reshape(-1)
        reduced_input = lax.dot_general(current_row_block, adapter_second_factor, (((1,), (1,)), ((), ())), preferred_element_type=jnp.float32).astype(jnp.bfloat16)
        stored_rows = stored_hidden_rows[expert_number].reshape(SOURCES * CAP, HIDDEN_UNITS)
        return per_expert_terms(current_row_block, routing_share, reduced_input, stored_rows, frozen_down_weight[expert_number], adapter_first_factor, expert_adapter_gate[expert_number])
    hidden_all, weight_all, first_factor_stack, second_factor_stack, gate_stack = lax.map(one_expert, jnp.arange(EXPERTS, dtype=jnp.int32))
    hidden_gradient = hidden_all.reshape(EXPERTS, SOURCES, CAP, HIDDEN_UNITS)
    by_source = weight_all.reshape(EXPERTS, SOURCES, CAP).transpose(1, 0, 2).reshape(SOURCES, EXPERTS * CAP)
    routing_gradient = jnp.take_along_axis(by_source, dest, axis=1).reshape(TOKENS, TOP)
    first_factor_gradient = lax.optimization_barrier(jnp.sum(first_factor_stack, axis=0))
    second_factor_gradient = lax.optimization_barrier(jnp.sum(second_factor_stack, axis=0))
    return (hidden_gradient, routing_gradient, first_factor_gradient, second_factor_gradient, gate_stack)
```

```python
import functools

import jax
import jax.numpy as jnp
from jax import lax
from jax.experimental import pallas as pl
from jax.experimental.pallas import tpu as pltpu
from jax.sharding import PartitionSpec as P

F32, BF16 = jnp.float32, jnp.bfloat16
VMEM_LIMIT = 40 * 1024 * 1024
ROWS = (((0,), (0,)), ((), ()))
LANES = (((1,), (1,)), ((), ()))
PLAIN = (((1,), (0,)), ((), ()))


def dot(a, b, dims):
    return lax.dot_general(a, b, dims, preferred_element_type=F32)


def params():
    return pltpu.CompilerParams(vmem_limit_bytes=VMEM_LIMIT)


def whole(count):
    return [pl.BlockSpec(memory_space=pltpu.VMEM)] * count


def scale_kernel(mantissa_ref, exponent_ref, low_ref, high_ref):
    exponents = exponent_ref[...]
    scale = jnp.zeros(exponents.shape, F32)
    for power in range(-2, 3):
        scale = scale + jnp.where(exponents == power, F32(2.0**power), F32(0.0))
    columns = scale.T
    half = low_ref.shape[0]
    width = mantissa_ref.shape[1] // exponents.shape[0]
    for block in range(exponents.shape[0]):
        lanes = slice(block * width, (block + 1) * width)
        piece = (mantissa_ref[:, lanes].astype(F32) * columns[:, block : block + 1]).astype(BF16)
        low_ref[:, lanes] = piece[:half]
        high_ref[:, lanes] = piece[half:]


def share_table(routes, weights, experts):
    expert = lax.broadcasted_iota(jnp.int32, (experts, routes.shape[1]), 0)
    table = jnp.zeros(expert.shape, F32)
    for k in range(routes.shape[0]):
        table = table + jnp.where(routes[k : k + 1] == expert, weights[k : k + 1], F32(0.0))
    return table


def pack_kernel(
    own_ref, low_ref, high_ref, second_ref, routes_ref, weights_ref, stored_ref, first_ref, gate_ref, out_ref
):
    devices, cap = stored_ref.shape[0], stored_ref.shape[1]
    rank = second_ref.shape[0]
    gate = gate_ref[own_ref[0]]
    reduced = jnp.concatenate(
        [dot(second_ref[...], low_ref[...], LANES), dot(second_ref[...], high_ref[...], LANES)], axis=1
    ).astype(BF16)
    table = share_table(routes_ref[...], weights_ref[...].astype(F32), devices).astype(BF16)
    first = first_ref[...]
    pad = jnp.zeros((rank, out_ref.shape[2] - cap), BF16)
    for peer in range(devices):
        out_ref[peer, 0:rank, :] = reduced
        pulled = (gate * dot(first, stored_ref[peer], LANES)).astype(BF16)
        out_ref[peer, rank : 2 * rank, :] = jnp.concatenate([pulled, pad], axis=1)
        out_ref[peer, 2 * rank :, :] = table


def slot_of(table):
    tokens = table.shape[1]
    earlier = lax.broadcasted_iota(jnp.int32, (tokens, tokens), 0) < lax.broadcasted_iota(
        jnp.int32, (tokens, tokens), 1
    )
    taken = jnp.where(table > 0, F32(1.0), F32(0.0)).astype(BF16)
    count = dot(taken, jnp.where(earlier, F32(1.0), F32(0.0)).astype(BF16), PLAIN)
    return jnp.where(table > 0, count, F32(-1.0)).astype(jnp.int32)


def take_row(table, row):
    rows = lax.broadcasted_iota(jnp.int32, table.shape, 0)
    return jnp.sum(jnp.where(rows == row, table, F32(0.0)), axis=0, keepdims=True)


def xor_mask(j):
    return ((j >> 3) & 1) | (((j >> 2) & 1) << 1) | (((j >> 1) & 1) << 2) | ((j & 1) << 3)


def low_rank_kernel(
    own_ref,
    got_ref,
    stored_ref,
    first_ref,
    gate_ref,
    routes_ref,
    weights_ref,
    low_ref,
    high_ref,
    out_ref,
    wide_ref,
    narrow_ref,
):
    devices, cap = stored_ref.shape[0], stored_ref.shape[1]
    own = own_ref[0]
    rank = first_ref.shape[0]
    tokens = got_ref.shape[2]
    gate = gate_ref[own]
    shares = jnp.concatenate(
        [take_row(got_ref[s, 2 * rank :, :].astype(F32), own) for s in range(devices)], axis=0
    )
    slots = slot_of(shares)
    place = lax.broadcasted_iota(jnp.int32, (tokens, tokens), 0)
    total = jnp.zeros((rank, stored_ref.shape[2]), F32)
    for s in range(devices):
        chosen = jnp.where(place == slots[s : s + 1], F32(1.0), F32(0.0)).astype(BF16)
        pushed = (got_ref[s, 0:rank, :].astype(F32) * shares[s : s + 1]).astype(BF16)
        by_slot = dot(pushed, chosen[:cap], LANES).astype(BF16)
        total = total + dot(by_slot, stored_ref[s], PLAIN)
    gate_term = jnp.sum(total * first_ref[...].astype(F32))
    total = gate * total
    narrow_ref[...] = jnp.zeros(narrow_ref.shape, F32)
    for i in range(2 * (total.shape[1] // 128)):
        narrow_ref[i] = total[(i % 2) * 16 : (i % 2) * 16 + 16, (i // 2) * 128 : (i // 2) * 128 + 128]
    lane = lax.broadcasted_iota(jnp.int32, (16, 128), 1)
    row = lax.broadcasted_iota(jnp.int32, (16, 128), 0)
    narrow_ref[devices - 1] = jnp.where((lane == own) & (row == 0), gate_term, F32(0.0))

    table = share_table(routes_ref[...], weights_ref[...].astype(F32), devices)
    mine = slot_of(table)
    pulled = jnp.zeros((rank, tokens), F32)
    for e in range(devices):
        weighted = jnp.where(place == mine[e : e + 1], table[e : e + 1], F32(0.0)).astype(BF16)
        pulled = pulled + dot(got_ref[e, rank : 2 * rank, :], weighted, PLAIN)
    coarse = pulled.astype(BF16)
    fine = (pulled - coarse.astype(F32)).astype(BF16)
    both = jnp.concatenate([coarse, fine], axis=0)
    half = low_ref.shape[0]
    result = dot(both[:, :half], low_ref[...], PLAIN) + dot(both[:, half:], high_ref[...], PLAIN)
    wide_ref[...] = result[:rank] + result[rank:]
    columns = wide_ref.shape[1] // devices
    for j in range(devices):
        chunk = own ^ xor_mask(j)
        for b in range(columns // 128):
            lanes = pl.ds(pl.multiple_of(chunk * columns + b * 128, 128), 128)
            out_ref[j, b * rank : (b + 1) * rank, :] = wide_ref[:, lanes]
        out_ref[j, 64:80, :] = narrow_ref[chunk]


def unpack_kernel(own_ref, got_ref, second_ref, first_ref, gate_ref, narrow_ref):
    devices = got_ref.shape[0]
    own = own_ref[0]
    rank = second_ref.shape[0]
    columns = second_ref.shape[1] // devices
    for j in range(devices):
        chunk = own ^ xor_mask(j)
        for b in range(columns // 128):
            lanes = pl.ds(pl.multiple_of(chunk * columns + b * 128, 128), 128)
            second_ref[:, lanes] = got_ref[j, b * rank : (b + 1) * rank, :]
        narrow_ref[chunk] = got_ref[j, 64:80, :]
    for i in range(2 * (first_ref.shape[1] // 128)):
        first_ref[(i % 2) * 16 : (i % 2) * 16 + 16, (i // 2) * 128 : (i // 2) * 128 + 128] = narrow_ref[i]
    gate_ref[...] = narrow_ref[devices - 1][0:8]


def expert_kernel(
    place_ref,
    gate_ref,
    a0_ref,
    a1_ref,
    b0_ref,
    b1_ref,
    weight_ref,
    other_weight_ref,
    stored_ref,
    other_stored_ref,
    first_ref,
    got_ref,
    *rest,
):
    hidden_ref, other_hidden_ref, dots_ref, rows_ref, sem = rest[-5:]
    step = pl.program_id(0)
    own, is_end = place_ref[0], place_ref[1]
    half = a0_ref.shape[0]
    cap = stored_ref.shape[1]
    rank = first_ref.shape[0]
    tokens = 2 * half

    @pl.when(step == 0)
    def _():
        def load(first_half, second_half):
            one = pltpu.make_async_copy(first_half, rows_ref.at[0:half], sem.at[0])
            two = pltpu.make_async_copy(second_half, rows_ref.at[half:tokens], sem.at[1])
            one.start()
            two.start()
            one.wait()
            two.wait()

        @pl.when(is_end == 1)
        def _():
            load(a0_ref, a1_ref)

        @pl.when(is_end == 0)
        def _():
            load(b0_ref, b1_ref)

        dots_ref[...] = jnp.zeros(dots_ref.shape, F32)

    def work(expert, row, weight_block, stored_block, hidden_block):
        share = take_row(got_ref[0, 2 * rank :, :].astype(F32), expert)
        slot = slot_of(jnp.broadcast_to(share, (8, tokens)))[0:1]
        chosen = jnp.where(
            lax.broadcasted_iota(jnp.int32, (cap, tokens), 0) == slot, F32(1.0), F32(0.0)
        ).astype(BF16)
        grad = dot(weight_block[0], rows_ref[...], LANES)
        grad = grad + gate_ref[expert] * dot(first_ref[...], got_ref[0, 0:rank, :], ROWS)
        by_token = dot(stored_block[0], chosen, ROWS)
        rows = lax.broadcasted_iota(jnp.int32, dots_ref.shape, 0)
        partial = jnp.sum(by_token * grad, axis=0, keepdims=True)
        dots_ref[...] += jnp.where(rows == row, partial, F32(0.0))
        hidden_block[0] = dot(chosen, (share * grad).astype(BF16), LANES).astype(BF16)

    steps = pl.num_programs(0) // 2

    @pl.when(step < steps)
    def _():
        work(own, 0, weight_ref, stored_ref, hidden_ref)

    @pl.when(step >= steps)
    def _():
        work(own ^ 1, 1, other_weight_ref, other_stored_ref, other_hidden_ref)


def expert_call(place, gate, buffers, weight, other_weight, stored, other_stored, first, got, turn, prev):
    devices, cap, hidden = stored.shape
    half, width = buffers[0].shape
    tile = 256
    steps = hidden // tile
    near = lambda n: jnp.minimum(n, steps - 1)
    far = lambda n: jnp.maximum(n - steps, 0)
    any_spec = pl.BlockSpec(memory_space=pl.ANY)
    in_specs = [any_spec] * 4 + [
        pl.BlockSpec((1, tile, width), lambda n, p, g: (0, near(n), 0)),
        pl.BlockSpec((1, tile, width), lambda n, p, g: (0, far(n), 0)),
        pl.BlockSpec((1, cap, tile), lambda n, p, g: (p[2], 0, near(n))),
        pl.BlockSpec((1, cap, tile), lambda n, p, g: (p[2], 0, far(n))),
        pl.BlockSpec((first.shape[0], tile), lambda n, p, g: (0, n % steps)),
        pl.BlockSpec((1,) + got.shape[1:], lambda n, p, g: (p[2], 0, 0)),
    ]
    operands = [place, gate, *buffers, weight, other_weight, stored, other_stored, first, got]
    aliases = {}
    if prev is not None:
        aliases = {len(operands): 0, len(operands) + 1: 1}
        operands += list(prev)
        in_specs += [any_spec, any_spec]
    flops = 2 * 2 * half * width * 2 * hidden
    return pl.pallas_call(
        expert_kernel,
        grid_spec=pltpu.PrefetchScalarGridSpec(
            num_scalar_prefetch=2,
            grid=(2 * steps,),
            in_specs=in_specs,
            out_specs=[
                pl.BlockSpec((1, cap, tile), lambda n, p, g: (p[2], 0, near(n))),
                pl.BlockSpec((1, cap, tile), lambda n, p, g: (turn, 0, far(n))),
                pl.BlockSpec((8, 2 * half), lambda n, p, g: (0, 0)),
            ],
            scratch_shapes=[pltpu.VMEM((2 * half, width), BF16), pltpu.SemaphoreType.DMA((2,))],
        ),
        out_shape=[
            jax.ShapeDtypeStruct((devices, cap, hidden), BF16),
            jax.ShapeDtypeStruct((devices // 2, cap, hidden), BF16),
            jax.ShapeDtypeStruct((8, 2 * half), F32),
        ],
        input_output_aliases=aliases,
        compiler_params=params(),
        cost_estimate=pl.CostEstimate(flops=flops, bytes_accessed=2 * 2 * hidden * width, transcendentals=0),
    )(*operands)


def finish_kernel(own_ref, masks, *refs):
    count = len(masks)
    dots, routes_ref, moved_ref = refs[:count], refs[count], refs[count + 1]
    routing_ref, hidden_ref, sem = refs[count + 3 :]
    own = own_ref[0]
    copies = []
    for k, mask in enumerate(masks):
        source = own ^ 1 ^ (mask << 1)
        copies.append(pltpu.make_async_copy(moved_ref.at[k], hidden_ref.at[source], sem.at[k]))
    for copy in copies:
        copy.start()
    routes = routes_ref[...]
    total = jnp.zeros(routes.shape, F32)
    for k, mask in enumerate(masks):
        for row in range(2):
            expert = own ^ (mask << 1) ^ row
            total = total + jnp.where(routes == expert, dots[k][row : row + 1, :], F32(0.0))
    routing_ref[...] = total
    for copy in copies:
        copy.wait()


def permutes():
    number = lambda z, x, c: (z * 2 + x) * 2 + c
    places = [(z, x, c) for z in range(4) for x in range(2) for c in range(2)]
    end = lambda z: z in (0, 3)
    return dict(
        near=[(number(z, x, c), number(z ^ 1, x, c)) for z, x, c in places],
        mid=[(number(z, x, c), number(3 - z, x, c)) for z, x, c in places if not end(z)],
        out=[(number(z, x, c), number(z ^ 1, x, c)) for z, x, c in places if not end(z)],
        inward=[(number(z, x, c), number(z ^ 1, x, c)) for z, x, c in places if end(z)],
        side=[(number(z, x, c), number(z, 1 - x, c)) for z, x, c in places],
        end_side=[(number(z, x, c), number(z, 1 - x, c)) for z, x, c in places if end(z)],
        mid_side=[(number(z, x, c), number(z, 1 - x, c)) for z, x, c in places if not end(z)],
    )


def xor_pairs(mask):
    return [(i, i ^ mask) for i in range(16)]


def send(value, pairs):
    return lax.ppermute(value, "ex", pairs)


def spread(low, high):
    to = permutes()
    own = [low, high]
    near = [send(h, to["near"]) for h in own]
    mid = [send(h, to["mid"]) for h in own]
    side = [send(h, to["side"]) for h in own]
    out2 = [send(h, to["out"]) for h in mid]
    mid2 = [send(h, to["mid"]) for h in near]
    in2 = [send(h, to["inward"]) for h in side]
    end1 = [send(h, to["end_side"]) for h in near]
    mids1 = [send(h, to["mid_side"]) for h in mid]
    out3 = [send(h, to["out"]) for h in mid2]
    end2 = [send(h, to["end_side"]) for h in out2]
    mids2 = [send(h, to["mid_side"]) for h in mid2]
    end3 = send(out3[0], to["end_side"])
    last = send(mids2[1], to["out"])
    return {
        0: (own, own),
        2: (near, near),
        1: (side, side),
        4: (out2, mid2),
        3: (end1, in2),
        6: (out3, mid),
        5: (end2, mids2),
        7: ([end3, last], mids1),
    }


def sum_over_group(value):
    for bit in (1, 2, 4, 8):
        half = value.shape[0] // 2
        value = value[:half] + send(value[half:], xor_pairs(bit))
    for bit in (8, 4, 2, 1):
        value = jnp.concatenate([value, send(value, xor_pairs(bit))], axis=0)
    return value


def small_body(
    gradient_mantissas,
    gradient_exponents,
    routes,
    routing_weight,
    stored_hidden_rows,
    frozen_down_weight,
    adapter_first_factor,
    adapter_second_factor,
    expert_adapter_gate,
):
    tokens, width = gradient_mantissas.shape
    stored = stored_hidden_rows[0]
    devices, cap, hidden = stored.shape
    rank = adapter_second_factor.shape[0]
    first = adapter_first_factor.T
    routes_t, weights_t = routes.T, routing_weight.T
    own = lax.axis_index("ex").astype(jnp.int32)
    own1 = own.reshape(1)
    z = own >> 2
    is_end = ((z == 0) | (z == 3)).astype(jnp.int32)
    smem = pl.BlockSpec(memory_space=pltpu.SMEM)

    other_weight = send(frozen_down_weight, xor_pairs(1))
    other_stored = send(stored, xor_pairs(1))
    low, high = pl.pallas_call(
        scale_kernel,
        in_specs=whole(2),
        out_specs=whole(2),
        out_shape=[jax.ShapeDtypeStruct((tokens // 2, width), BF16)] * 2,
        compiler_params=params(),
    )(gradient_mantissas, gradient_exponents.T)
    buffers = spread(low, high)

    packed = pl.pallas_call(
        pack_kernel,
        in_specs=[smem] + whole(7) + [smem],
        out_specs=pl.BlockSpec(memory_space=pltpu.VMEM),
        out_shape=jax.ShapeDtypeStruct((devices, 2 * rank + devices, tokens), BF16),
        compiler_params=params(),
    )(own1, low, high, adapter_second_factor, routes_t, weights_t, stored, first, expert_adapter_gate)
    got = lax.all_to_all(packed, "ex", split_axis=0, concat_axis=0, tiled=True)
    partial = pl.pallas_call(
        low_rank_kernel,
        in_specs=[smem] + whole(3) + [smem] + whole(4),
        out_specs=pl.BlockSpec(memory_space=pltpu.VMEM),
        out_shape=jax.ShapeDtypeStruct((devices, 80, 128), F32),
        scratch_shapes=[pltpu.VMEM((rank, width), F32), pltpu.VMEM((devices, 16, 128), F32)],
        compiler_params=params(),
    )(own1, got, stored, first, expert_adapter_gate, routes_t, weights_t, low, high)
    summed = sum_over_group(partial)
    second_grad, first_grad, gate_grad = pl.pallas_call(
        unpack_kernel,
        in_specs=[smem] + whole(1),
        out_specs=whole(3),
        out_shape=[
            jax.ShapeDtypeStruct((rank, width), F32),
            jax.ShapeDtypeStruct((rank, hidden), F32),
            jax.ShapeDtypeStruct((8, 128), F32),
        ],
        scratch_shapes=[pltpu.VMEM((devices, 16, 128), F32)],
        compiler_params=params(),
    )(own1, summed)

    masks = (0, 2, 1, 4, 3, 6, 5, 7)
    dots, prev = [], None
    for turn, mask in enumerate(masks):
        place = jnp.stack([own, is_end, own ^ (mask << 1)])
        as_end, as_mid = buffers[mask]
        *prev, dot_rows = expert_call(
            place,
            expert_adapter_gate,
            [*as_end, *as_mid],
            frozen_down_weight,
            other_weight,
            stored,
            other_stored,
            first,
            got,
            turn,
            prev,
        )
        dots.append(send(dot_rows, xor_pairs(mask << 1)) if mask else dot_rows)
    hidden_part, other_part = prev
    moved = send(other_part, xor_pairs(1))
    any_spec = pl.BlockSpec(memory_space=pl.ANY)
    routing_t, hidden_gradient = pl.pallas_call(
        lambda own_ref, *refs: finish_kernel(own_ref, masks, *refs),
        in_specs=[smem] + whole(len(masks) + 1) + [any_spec, any_spec],
        out_specs=[pl.BlockSpec(memory_space=pltpu.VMEM), any_spec],
        out_shape=[
            jax.ShapeDtypeStruct(routes_t.shape, F32),
            jax.ShapeDtypeStruct((devices, cap, hidden), BF16),
        ],
        input_output_aliases={len(masks) + 3: 1},
        scratch_shapes=[pltpu.SemaphoreType.DMA((len(masks),))],
        compiler_params=params(),
    )(own1, *dots, routes_t, moved, hidden_part)
    return (
        hidden_gradient[None],
        routing_t.T,
        first_grad.T,
        second_grad,
        gate_grad[0, :devices],
    )


def block_scale(gradient_exponents):
    scaling = jnp.zeros(gradient_exponents.shape, jnp.float32)
    for exponent in range(-2, 3):
        scaling = scaling + jnp.where(
            gradient_exponents == exponent, jnp.float32(2.0**exponent), jnp.float32(0.0)
        )
    return scaling


def expand_grad(gradient_mantissas, gradient_exponents):
    blocks = gradient_exponents.shape[1]
    scaling = block_scale(gradient_exponents)
    widened = (
        gradient_mantissas.astype(jnp.float32).reshape(gradient_mantissas.shape[0], blocks, -1)
        * scaling[:, :, None]
    )
    return widened.reshape(gradient_mantissas.shape).astype(jnp.bfloat16)


def slot_table(route_block, experts, capacity):
    flat_routes = route_block.reshape(-1)
    onehot = (flat_routes[:, None] == jnp.arange(experts, dtype=jnp.int32)[None, :]).astype(
        jnp.int32
    )
    running = jnp.cumsum(onehot, axis=0) - 1
    slot_index = jnp.sum(running * onehot, axis=1)
    return flat_routes * capacity + slot_index


def reduced_projection(current_row_block, adapter_second_factor):
    return lax.dot_general(
        current_row_block,
        adapter_second_factor,
        (((1,), (1,)), ((), ())),
        preferred_element_type=jnp.float32,
    ).astype(jnp.bfloat16)


def per_expert_terms(
    current_row_block,
    routing_share,
    reduced_input,
    stored_rows,
    expert_down_matrix,
    adapter_first_factor,
    expert_gate_value,
):
    contract_dimensions = (((1,), (1,)), ((), ()))
    base_term = lax.dot_general(
        current_row_block,
        expert_down_matrix,
        contract_dimensions,
        preferred_element_type=jnp.float32,
    )
    adapter_side_term = lax.dot_general(
        reduced_input, adapter_first_factor, contract_dimensions, preferred_element_type=jnp.float32
    )
    combined = base_term + expert_gate_value * adapter_side_term
    share_col = routing_share.astype(jnp.float32)[:, None]
    hidden_gradient = (share_col * combined).astype(jnp.bfloat16)
    weight_grad = jnp.sum(stored_rows.astype(jnp.float32) * combined, axis=1)
    low_float = reduced_input.astype(jnp.float32)
    rows_dims = (((0,), (0,)), ((), ()))
    pushed = (expert_gate_value * share_col * low_float).astype(jnp.bfloat16)
    a_grad = lax.dot_general(stored_rows, pushed, rows_dims, preferred_element_type=jnp.float32)
    reduced_rank_rows = jnp.dot(
        stored_rows, adapter_first_factor, preferred_element_type=jnp.float32
    )
    pulled = (expert_gate_value * share_col * reduced_rank_rows).astype(jnp.bfloat16)
    b_grad = lax.dot_general(
        pulled, current_row_block, rows_dims, preferred_element_type=jnp.float32
    )
    gate_term = jnp.sum(
        routing_share.astype(jnp.float32) * jnp.sum(reduced_rank_rows * low_float, axis=1)
    )
    return (hidden_gradient, weight_grad, a_grad, b_grad, gate_term)


def body(
    gradient_mantissas,
    gradient_exponents,
    routes,
    routing_weight,
    stored_hidden_rows,
    frozen_down_weight,
    adapter_first_factor,
    adapter_second_factor,
    expert_adapter_gate,
):
    experts = expert_adapter_gate.shape[0]
    sources = stored_hidden_rows.shape[1]
    capacity = stored_hidden_rows.shape[2]
    hidden_width = stored_hidden_rows.shape[3]
    tok_count, top_count = routes.shape
    slots_all = experts * capacity
    grad_out = expand_grad(gradient_mantissas, gradient_exponents)
    dest = slot_table(routes, experts, capacity)
    token_ids = jnp.arange(tok_count * top_count, dtype=jnp.int32) // top_count
    token_of = jnp.zeros((slots_all,), jnp.int32).at[dest].set(token_ids)
    share_send = (
        jnp.zeros((slots_all,), jnp.bfloat16)
        .at[dest]
        .set(routing_weight.reshape(-1))
        .reshape(experts, capacity)
    )
    row_send = grad_out[token_of].reshape(experts, capacity, -1)
    received_rows = sources * capacity
    token_low = reduced_projection(grad_out, adapter_second_factor)
    low_send = token_low[token_of].reshape(experts, capacity, -1)
    row_recv, share_recv, low_recv = (
        lax.all_to_all(row_send, "ex", split_axis=0, concat_axis=0, tiled=True),
        lax.all_to_all(share_send, "ex", split_axis=0, concat_axis=0, tiled=True),
        lax.all_to_all(low_send, "ex", split_axis=0, concat_axis=0, tiled=True),
    )
    current_row_block = row_recv.reshape(received_rows, -1)
    reduced_input = low_recv.reshape(received_rows, -1)
    routing_share = share_recv.reshape(received_rows)
    stored_rows = stored_hidden_rows.reshape(received_rows, hidden_width)
    expert_down_matrix = frozen_down_weight[0]
    own_index = lax.axis_index("ex")
    expert_gate_value = lax.dynamic_index_in_dim(expert_adapter_gate, own_index, 0, keepdims=False)
    hidden_gradient, weight_grad, a_grad, b_grad, gate_term = per_expert_terms(
        current_row_block,
        routing_share,
        reduced_input,
        stored_rows,
        expert_down_matrix,
        adapter_first_factor,
        expert_gate_value,
    )
    returned = lax.all_to_all(
        weight_grad.reshape(sources, capacity), "ex", split_axis=0, concat_axis=0, tiled=True
    )
    routing_gradient = returned.reshape(-1)[dest].reshape(tok_count, top_count)
    own_gate = (jnp.arange(experts, dtype=jnp.int32) == own_index).astype(jnp.float32) * gate_term
    a_total, b_total, gate_total = lax.psum((a_grad, b_grad, own_gate), "ex")
    hidden_out = hidden_gradient.reshape(1, sources, capacity, hidden_width)
    return (hidden_out, routing_gradient, a_total, b_total, gate_total)


def solution(mesh):
    return jax.shard_map(
        small_body if mesh.shape["ex"] == 16 else body,
        mesh=mesh,
        in_specs=(
            P(("groups", "ex"), None),
            P(("groups", "ex"), None),
            P(("groups", "ex"), None),
            P(("groups", "ex"), None),
            P(("groups", "ex"), None, None, None),
            P("ex", None, None),
            P(),
            P(),
            P(),
        ),
        out_specs=(
            P(("groups", "ex"), None, None, None),
            P(("groups", "ex"), None),
            P("groups", None),
            P("groups", None),
            P("groups"),
        ),
        check_vma=False,
    )
```

```python
import functools

import jax
import jax.numpy as jnp
from jax import lax
from jax.experimental import pallas as pl
from jax.experimental.pallas import tpu as pltpu
from jax.sharding import PartitionSpec as P

F32, BF16 = jnp.float32, jnp.bfloat16
VMEM_LIMIT = 16 * 1024 * 1024
BIG_LIMIT = 59 * 1024 * 1024
TILE, AHEAD = 384, 2
ROWS = (((0,), (0,)), ((), ()))
LANES = (((1,), (1,)), ((), ()))
PLAIN = (((1,), (0,)), ((), ()))


def dot(a, b, dims):
    return lax.dot_general(a, b, dims, preferred_element_type=F32)


SMALL = pl.CostEstimate(flops=1000000, bytes_accessed=10000, transcendentals=0)

LARGE = pl.CostEstimate(flops=30000000000, bytes_accessed=10000, transcendentals=0)


def params(limit=VMEM_LIMIT):
    return pltpu.CompilerParams(vmem_limit_bytes=limit)


def whole(count):
    return [pl.BlockSpec(memory_space=pltpu.VMEM)] * count


def scale_kernel(mantissa_ref, exponent_ref, rows_ref):
    exponents = exponent_ref[...]
    scale = jnp.zeros(exponents.shape, F32)
    for power in range(-2, 3):
        scale = scale + jnp.where(exponents == power, F32(2.0**power), F32(0.0))
    columns = scale.T
    width = mantissa_ref.shape[1] // exponents.shape[0]
    for block in range(exponents.shape[0]):
        lanes = slice(block * width, (block + 1) * width)
        rows_ref[:, lanes] = (mantissa_ref[:, lanes].astype(F32) * columns[:, block : block + 1]).astype(BF16)


def share_table(routes, weights, experts):
    expert = lax.broadcasted_iota(jnp.int32, (experts, routes.shape[1]), 0)
    table = jnp.zeros(expert.shape, F32)
    for k in range(routes.shape[0]):
        table = table + jnp.where(routes[k : k + 1] == expert, weights[k : k + 1], F32(0.0))
    return table


def pack_kernel(
    own_ref, rows_ref, second_ref, routes_ref, weights_ref, stored_ref, first_ref, gate_ref, out_ref
):
    devices, cap = stored_ref.shape[0], stored_ref.shape[1]
    rank = second_ref.shape[0]
    gate = gate_ref[own_ref[0]]
    reduced = dot(second_ref[...], rows_ref[...], LANES).astype(BF16)
    table = share_table(routes_ref[...], weights_ref[...].astype(F32), devices).astype(BF16)
    first = first_ref[...]
    pad = jnp.zeros((rank, out_ref.shape[2] - cap), BF16)
    for peer in range(devices):
        out_ref[peer, 0:rank, :] = reduced
        pulled = (gate * dot(first, stored_ref[peer], LANES)).astype(BF16)
        out_ref[peer, rank : 2 * rank, :] = jnp.concatenate([pulled, pad], axis=1)
        out_ref[peer, 2 * rank :, :] = table


def slot_of(table):
    tokens = table.shape[1]
    earlier = lax.broadcasted_iota(jnp.int32, (tokens, tokens), 0) < lax.broadcasted_iota(
        jnp.int32, (tokens, tokens), 1
    )
    taken = jnp.where(table > 0, F32(1.0), F32(0.0)).astype(BF16)
    count = dot(taken, jnp.where(earlier, F32(1.0), F32(0.0)).astype(BF16), PLAIN)
    return jnp.where(table > 0, count, F32(-1.0)).astype(jnp.int32)


def take_row(table, row):
    rows = lax.broadcasted_iota(jnp.int32, table.shape, 0)
    return jnp.sum(jnp.where(rows == row, table, F32(0.0)), axis=0, keepdims=True)


def chunk_of(j, own, devices):
    half = devices // 2
    return 2 * j + (own & 1) if j < half else 2 * (j - half) + ((own & 1) ^ 1)


def low_rank_kernel(
    own_ref,
    got_ref,
    stored_ref,
    first_ref,
    gate_ref,
    routes_ref,
    weights_ref,
    rows_ref,
    out_ref,
    wide_ref,
    narrow_ref,
):
    devices, cap = stored_ref.shape[0], stored_ref.shape[1]
    own = own_ref[0]
    rank = first_ref.shape[0]
    tokens = got_ref.shape[2]
    gate = gate_ref[own]
    shares = jnp.concatenate(
        [take_row(got_ref[s, 2 * rank :, :].astype(F32), own) for s in range(devices)], axis=0
    )
    slots = slot_of(shares)
    place = lax.broadcasted_iota(jnp.int32, (tokens, tokens), 0)
    total = jnp.zeros((rank, stored_ref.shape[2]), F32)
    for s in range(devices):
        chosen = jnp.where(place == slots[s : s + 1], F32(1.0), F32(0.0)).astype(BF16)
        pushed = (got_ref[s, 0:rank, :].astype(F32) * shares[s : s + 1]).astype(BF16)
        by_slot = dot(pushed, chosen[:cap], LANES).astype(BF16)
        total = total + dot(by_slot, stored_ref[s], PLAIN)
    gate_term = jnp.sum(total * first_ref[...].astype(F32))
    total = gate * total
    narrow_ref[...] = jnp.zeros(narrow_ref.shape, F32)
    for i in range(2 * (total.shape[1] // 128)):
        narrow_ref[i] = total[(i % 2) * 16 : (i % 2) * 16 + 16, (i // 2) * 128 : (i // 2) * 128 + 128]
    lane = lax.broadcasted_iota(jnp.int32, (16, 128), 1)
    row = lax.broadcasted_iota(jnp.int32, (16, 128), 0)
    narrow_ref[devices - 1] = jnp.where((lane == own) & (row == 0), gate_term, F32(0.0))

    table = share_table(routes_ref[...], weights_ref[...].astype(F32), devices)
    mine = slot_of(table)
    pulled = jnp.zeros((rank, tokens), F32)
    for e in range(devices):
        weighted = jnp.where(place == mine[e : e + 1], table[e : e + 1], F32(0.0)).astype(BF16)
        pulled = pulled + dot(got_ref[e, rank : 2 * rank, :], weighted, PLAIN)
    coarse = pulled.astype(BF16)
    fine = (pulled - coarse.astype(F32)).astype(BF16)
    both = jnp.concatenate([coarse, fine], axis=0)
    result = dot(both, rows_ref[...], PLAIN)
    wide_ref[...] = result[:rank] + result[rank:]
    columns = wide_ref.shape[1] // devices
    for j in range(devices):
        chunk = chunk_of(j, own, devices)
        for b in range(columns // 128):
            lanes = pl.ds(pl.multiple_of(chunk * columns + b * 128, 128), 128)
            out_ref[j, b * rank : (b + 1) * rank, :] = wide_ref[:, lanes]
        out_ref[j, 64:80, :] = narrow_ref[chunk]


def unpack_kernel(own_ref, got_ref, second_ref, first_ref, gate_ref, narrow_ref):
    devices = got_ref.shape[0]
    own = own_ref[0]
    rank = second_ref.shape[0]
    columns = second_ref.shape[1] // devices
    for j in range(devices):
        chunk = chunk_of(j, own, devices)
        for b in range(columns // 128):
            lanes = pl.ds(pl.multiple_of(chunk * columns + b * 128, 128), 128)
            second_ref[:, lanes] = got_ref[j, b * rank : (b + 1) * rank, :].astype(F32)
        narrow_ref[chunk] = got_ref[j, 64:80, :].astype(F32)
    for i in range(2 * (first_ref.shape[1] // 128)):
        first_ref[(i % 2) * 16 : (i % 2) * 16 + 16, (i // 2) * 128 : (i // 2) * 128 + 128] = narrow_ref[i]
    gate_ref[...] = narrow_ref[devices - 1][0:8]


def expert_kernel(
    place_ref,
    gate_ref,
    weight_ref,
    other_weight_ref,
    stored_ref,
    other_stored_ref,
    first_ref,
    got_ref,
    *rest,
    layout,
    slot,
):
    hidden_out, other_out, dots_ref, rows_ref, held_ref, kept_ref, hidden_ref = rest[-15:-8]
    adapted_ref, chosen_ref, shares_ref, results_ref, load_sem, held_sem, kept_sem, write_sem = rest[-8:]
    tile = held_ref.shape[1]
    tiles = weight_ref.shape[1] // tile
    own, is_end = place_ref[0], place_ref[1]
    cap = stored_ref.shape[1]
    rank = first_ref.shape[0]
    units = len(layout)
    tokens = rows_ref.shape[0] // units
    choices, taken = ([], []), 0
    for unit, counts in enumerate(layout):
        for role, count in enumerate(counts):
            begin = unit * tokens
            for k in range(count):
                piece = rest[taken]
                target = rows_ref.at[begin : begin + piece.shape[0]]
                choices[role].append(pltpu.make_async_copy(piece, target, load_sem.at[len(choices[role])]))
                begin += piece.shape[0]
                taken += 1
    for flag, copies in ((1, choices[0]), (0, choices[1])):

        @pl.when(is_end == flag)
        def _():
            for copy in copies:
                copy.start()

    kept = []
    for k, stored in enumerate((stored_ref, other_stored_ref)):
        for unit in range(units):
            kept.append(
                pltpu.make_async_copy(
                    stored.at[place_ref[2 + unit]], kept_ref.at[k, unit], kept_sem.at[k * units + unit]
                )
            )
            kept[-1].start()

    def load(n):
        begin = pl.multiple_of(n % tiles * tile, tile)
        at = lambda weight: pltpu.make_async_copy(weight.at[0, pl.ds(begin, tile)], held_ref.at[n], held_sem.at[n])

        @pl.when(n < tiles)
        def _():
            at(weight_ref).start()

        @pl.when(n >= tiles)
        def _():
            at(other_weight_ref).start()

    for n in range(AHEAD):
        load(jnp.int32(n))

    place = lax.broadcasted_iota(jnp.int32, (cap, tokens), 0)
    for unit in range(units):
        source = place_ref[2 + unit]
        table = got_ref[source, 2 * rank :, :].astype(F32)
        shares = jnp.concatenate(
            [take_row(table, own), take_row(table, own ^ 1), jnp.zeros((6, tokens), F32)], axis=0
        )
        slots = slot_of(shares)
        columns = shares.T
        adapted_ref[unit] = dot(got_ref[source, 0:rank, :], first_ref[...], ROWS)
        for k in range(2):
            chosen_ref[k, unit] = jnp.where(place == slots[k : k + 1], F32(1.0), F32(0.0)).astype(BF16)
            shares_ref[k, unit] = jnp.broadcast_to(columns[:, k : k + 1], (tokens, 128))
    results_ref[...] = jnp.zeros(results_ref.shape, F32)
    for copy in kept:
        copy.wait()
    for flag, copies in ((1, choices[0]), (0, choices[1])):

        @pl.when(is_end == flag)
        def _():
            for copy in copies:
                copy.wait()

    lane = lax.broadcasted_iota(jnp.int32, (tokens, 128), 1)

    @pl.loop(0, 2 * tiles)
    def _(n):
        @pl.when(n + AHEAD < 2 * tiles)
        def _():
            load(n + AHEAD)

        k = n // tiles
        span = pl.ds(pl.multiple_of(n % tiles * tile, tile), tile)
        pltpu.make_async_copy(weight_ref.at[0, 0:tile], held_ref.at[n], held_sem.at[n]).wait()
        grads = dot(rows_ref[...], held_ref[n], LANES)
        gate = gate_ref[own ^ k]
        for unit in range(units):
            chosen = chosen_ref[k, unit]
            by_token = dot(chosen, kept_ref[k, unit, :, span], ROWS)
            grad = grads[unit * tokens : (unit + 1) * tokens] + gate * adapted_ref[unit, :, span]
            partial = jnp.sum(by_token * grad, axis=1, keepdims=True)
            results_ref[unit] += jnp.where(lane == k, partial, F32(0.0))
            shared = dot(chosen, (shares_ref[k, unit, :, 0:1] * grad).astype(BF16), PLAIN)
            hidden_ref[k, unit, :, span] = shared.astype(BF16)

    writes = []
    for unit in range(units):
        for k, target in enumerate((hidden_out.at[place_ref[2 + unit]], other_out.at[slot + unit])):
            writes.append(pltpu.make_async_copy(hidden_ref.at[k, unit], target, write_sem.at[len(writes)]))
            writes[-1].start()
    for unit in range(units):
        dots_ref[unit] = results_ref[unit].T[:8]
    for copy in writes:
        copy.wait()


def expert_call(place, gate, weight, other_weight, stored, other_stored, first, got, buffers, hidden, other, slot):
    devices, cap, width_hidden = stored.shape
    layout = [(len(as_end), len(as_mid)) for as_end, as_mid in buffers]
    pieces = [piece for pair in buffers for side in pair for piece in side]
    width = pieces[0].shape[1]
    tokens = got.shape[2]
    units = len(buffers)
    any_spec = pl.BlockSpec(memory_space=pl.ANY)
    smem = pl.BlockSpec(memory_space=pltpu.SMEM)
    operands = [place, gate, weight, other_weight, stored, other_stored, first, got, *pieces]
    in_specs = [smem] * 2 + [any_spec] * 4 + whole(2) + [any_spec] * len(pieces)
    aliases, sizes = {}, []
    for number, value in enumerate((hidden, other)):
        if isinstance(value, int):
            sizes.append(value)
        else:
            sizes.append(value.shape[0])
            aliases[len(operands)] = number
            operands.append(value)
            in_specs.append(any_spec)
    loads = max(sum(counts[role] for counts in layout) for role in range(2))
    return pl.pallas_call(
        functools.partial(expert_kernel, layout=layout, slot=slot),
        in_specs=in_specs,
        out_specs=[any_spec, any_spec, pl.BlockSpec(memory_space=pltpu.VMEM)],
        out_shape=[
            jax.ShapeDtypeStruct((sizes[0], cap, width_hidden), BF16),
            jax.ShapeDtypeStruct((sizes[1], cap, width_hidden), BF16),
            jax.ShapeDtypeStruct((units, 8, tokens), F32),
        ],
        scratch_shapes=[
            pltpu.VMEM((units * tokens, width), BF16),
            pltpu.VMEM((2 * width_hidden // TILE, TILE, width), BF16),
            pltpu.VMEM((2, units, cap, width_hidden), BF16),
            pltpu.VMEM((2, units, cap, width_hidden), BF16),
            pltpu.VMEM((units, tokens, width_hidden), F32),
            pltpu.VMEM((2, units, cap, tokens), BF16),
            pltpu.VMEM((2, units, tokens, 128), F32),
            pltpu.VMEM((units, tokens, 128), F32),
            pltpu.SemaphoreType.DMA((loads,)),
            pltpu.SemaphoreType.DMA((2 * width_hidden // TILE,)),
            pltpu.SemaphoreType.DMA((2 * units,)),
            pltpu.SemaphoreType.DMA((2 * units,)),
        ],
        input_output_aliases=aliases,
        compiler_params=params(BIG_LIMIT),
        cost_estimate=SMALL,
    )(*operands)


def place_kernel(own_ref, *refs, masks):
    hidden_ref, sem = refs[-2:]
    copies = []
    for moved_ref, turns in zip(refs, masks):
        for k, mask in enumerate(turns):
            source = own_ref[0] ^ 1 ^ (mask << 1)
            copies.append(pltpu.make_async_copy(moved_ref.at[k], hidden_ref.at[source], sem.at[len(copies)]))
    for copy in copies:
        copy.start()
    for copy in copies:
        copy.wait()


def place_call(own1, moved, hidden, masks):
    any_spec = pl.BlockSpec(memory_space=pl.ANY)
    return pl.pallas_call(
        functools.partial(place_kernel, masks=masks),
        in_specs=[pl.BlockSpec(memory_space=pltpu.SMEM)] + whole(len(moved)) + [any_spec],
        out_specs=any_spec,
        out_shape=jax.ShapeDtypeStruct(hidden.shape, hidden.dtype),
        input_output_aliases={1 + len(moved): 0},
        scratch_shapes=[pltpu.SemaphoreType.DMA((sum(len(turns) for turns in masks),))],
        compiler_params=params(),
        cost_estimate=SMALL,
    )(own1, *moved, hidden)


def finish_kernel(own_ref, *refs, masks):
    count = len(masks)
    dots, routes_ref, moved_ref = refs[:count], refs[count], refs[count + 1]
    routing_ref, hidden_ref, sem = refs[count + 3 :]
    own = own_ref[0]
    copy = pltpu.make_async_copy(moved_ref.at[0], hidden_ref.at[own ^ 1 ^ (masks[-1] << 1)], sem)
    copy.start()
    routes = routes_ref[...]
    total = jnp.zeros(routes.shape, F32)
    for k, mask in enumerate(masks):
        for row in range(2):
            expert = own ^ (mask << 1) ^ row
            total = total + jnp.where(routes == expert, dots[k][row : row + 1, :], F32(0.0))
    routing_ref[...] = total
    copy.wait()


def permutes():
    number = lambda z, x, c: (z * 2 + x) * 2 + c
    places = [(z, x, c) for z in range(4) for x in range(2) for c in range(2)]
    end = lambda z: z in (0, 3)
    return dict(
        near=[(number(z, x, c), number(z ^ 1, x, c)) for z, x, c in places],
        mid=[(number(z, x, c), number(3 - z, x, c)) for z, x, c in places if not end(z)],
        out=[(number(z, x, c), number(z ^ 1, x, c)) for z, x, c in places if not end(z)],
        side=[(number(z, x, c), number(z, 1 - x, c)) for z, x, c in places],
        end_side=[(number(z, x, c), number(z, 1 - x, c)) for z, x, c in places if end(z)],
    )


def xor_pairs(mask):
    return [(i, i ^ mask) for i in range(16)]


def send(value, pairs):
    return lax.ppermute(value, "ex", pairs)


def then(value, *earlier):
    return lax.optimization_barrier((value, *earlier))[0]


def small_body(
    gradient_mantissas,
    gradient_exponents,
    routes,
    routing_weight,
    stored_hidden_rows,
    frozen_down_weight,
    adapter_first_factor,
    adapter_second_factor,
    expert_adapter_gate,
):
    tokens, width = gradient_mantissas.shape
    stored = stored_hidden_rows[0]
    devices, cap, hidden = stored.shape
    rank = adapter_second_factor.shape[0]
    first = adapter_first_factor.T
    routes_t, weights_t = routes.T, routing_weight.T
    own = lax.axis_index("ex").astype(jnp.int32)
    own1 = own.reshape(1)
    z = own >> 2
    is_end = ((z == 0) | (z == 3)).astype(jnp.int32)

    smem = pl.BlockSpec(memory_space=pltpu.SMEM)
    vmem = pl.BlockSpec(memory_space=pltpu.VMEM)
    any_spec = pl.BlockSpec(memory_space=pl.ANY)
    to = permutes()
    pick = lambda as_end, as_mid: jnp.where(is_end == 1, as_end, as_mid)

    smem = pl.BlockSpec(memory_space=pltpu.SMEM)
    vmem = pl.BlockSpec(memory_space=pltpu.VMEM)
    any_spec = pl.BlockSpec(memory_space=pl.ANY)
    to = permutes()
    pick = lambda as_end, as_mid: jnp.where(is_end == 1, as_end, as_mid)

    other_weight = send(frozen_down_weight, xor_pairs(1))
    other_stored = send(stored, xor_pairs(1))
    rows = pl.pallas_call(
        scale_kernel,
        in_specs=whole(2),
        out_specs=vmem,
        out_shape=jax.ShapeDtypeStruct((tokens, width), BF16),
        compiler_params=params(),
        cost_estimate=SMALL,
    )(gradient_mantissas, gradient_exponents.T)
    masks = (0, 2, 1, 4, 3, 6, 5, 7)
    final = len(masks) - 1
    half = tokens // 2
    dots, hidden_part, other_part = [], devices, 5

    def experts(count, buffers, *earlier):
        nonlocal hidden_part, other_part
        begin = len(dots)
        turns = masks[begin : begin + count]
        place = jnp.stack([own, is_end] + [own ^ (mask << 1) for mask in turns])
        hidden_part, other_part, found = expert_call(
            then(place, *earlier),
            expert_adapter_gate,
            frozen_down_weight,
            other_weight,
            stored,
            other_stored,
            first,
            got,
            buffers,
            hidden_part,
            other_part,
            begin if begin < 5 else 0,
        )
        for k, mask in enumerate(turns):
            dots.append(send(found[k], xor_pairs(mask << 1)) if mask else found[k])
        return found

    near, side, mid = send(rows, to["near"]), send(rows, to["side"]), send(rows, to["mid"])
    packed = pl.pallas_call(
        pack_kernel,
        in_specs=[smem] + whole(6) + [smem],
        out_specs=vmem,
        out_shape=jax.ShapeDtypeStruct((devices, 2 * rank + devices, tokens), BF16),
        compiler_params=params(),
        cost_estimate=SMALL,
    )(
        then(own1, other_stored),
        rows,
        adapter_second_factor,
        routes_t,
        weights_t,
        stored,
        first,
        expert_adapter_gate,
    )
    got = lax.all_to_all(packed, "ex", split_axis=0, concat_axis=0, tiled=True)
    near, side, mid, _, _ = lax.optimization_barrier((near, side, mid, got, other_weight))
    near2 = send(pick(side, mid), to["near"])
    side2 = send(pick(near, mid), to["side"])
    mid2 = send(near, to["mid"])
    partial = pl.pallas_call(
        low_rank_kernel,
        in_specs=[smem] + whole(3) + [smem] + whole(3),
        out_specs=vmem,
        out_shape=jax.ShapeDtypeStruct((devices, 80, 128), F32),
        scratch_shapes=[pltpu.VMEM((rank, width), F32), pltpu.VMEM((devices, 16, 128), F32)],
        compiler_params=params(),
        cost_estimate=SMALL,
    )(then(own1, near, side, mid), got, stored, first, expert_adapter_gate, routes_t, weights_t, rows)
    lanes = [[2 * chip + core for chip in range(devices // 2)] for core in range(2)]
    among_lane = lambda value: lax.all_to_all(
        value, "ex", split_axis=0, concat_axis=0, axis_index_groups=lanes, tiled=True
    )
    found = experts(3, [([rows], [rows]), ([near], [near]), ([side], [side])], partial, near, side, mid)
    near2, mid2, side2, partial, _ = lax.optimization_barrier((near2, mid2, side2, partial, found))
    pair = (partial[: devices // 2] + send(partial[devices // 2 :], xor_pairs(1))).astype(BF16)
    parts = among_lane(pair)
    near3 = send(mid2, to["out"])
    side3 = send(pick(near2, mid2), to["side"])
    found = experts(2, [([near2], [mid2]), ([side2], [near2])], near2, side2, mid2)
    summed = jnp.sum(then(parts, found).astype(F32), axis=0).astype(BF16)
    near3, side3, _, summed = lax.optimization_barrier((near3, side3, found, summed))
    summed = among_lane(jnp.broadcast_to(summed[None], (devices // 2, 80, 128)))
    last = [send(near3[:half], to["end_side"]), send(side3[half:], to["out"])]
    moved, other_part = [send(then(other_part, found), xor_pairs(1))], 2
    found = experts(2, [([near3], [mid]), ([side3], [side3])], near3, side3, moved[0])
    summed = jnp.concatenate([summed, send(summed, xor_pairs(1))], axis=0)
    moved.append(send(other_part, xor_pairs(1)))
    other_part = 1
    found = experts(1, [(last, [side2])], *last)
    last_moved = send(other_part, xor_pairs(1))
    second_grad, first_grad, gate_grad = pl.pallas_call(
        unpack_kernel,
        in_specs=[smem] + whole(1),
        out_specs=whole(3),
        out_shape=[
            jax.ShapeDtypeStruct((rank, width), F32),
            jax.ShapeDtypeStruct((rank, hidden), F32),
            jax.ShapeDtypeStruct((8, 128), F32),
        ],
        scratch_shapes=[pltpu.VMEM((devices, 16, 128), F32)],
        compiler_params=params(),
        cost_estimate=SMALL,
    )(then(own1, found), summed)
    hidden_part = place_call(own1, moved, hidden_part, (masks[:5], masks[5:final]))
    moved = last_moved
    routing_t, hidden_gradient = pl.pallas_call(
        functools.partial(finish_kernel, masks=masks),
        in_specs=[smem] + whole(len(masks) + 2) + [any_spec],
        out_specs=[vmem, any_spec],
        out_shape=[
            jax.ShapeDtypeStruct(routes_t.shape, F32),
            jax.ShapeDtypeStruct((devices, cap, hidden), BF16),
        ],
        input_output_aliases={len(masks) + 3: 1},
        scratch_shapes=[pltpu.SemaphoreType.DMA],
        compiler_params=params(),
        cost_estimate=SMALL,
    )(own1, *dots, routes_t, moved, hidden_part)
    return (
        hidden_gradient[None],
        routing_t.T,
        first_grad.T,
        second_grad,
        gate_grad[0, :devices],
    )


def block_scale(gradient_exponents):
    scaling = jnp.zeros(gradient_exponents.shape, jnp.float32)
    for exponent in range(-2, 3):
        scaling = scaling + jnp.where(
            gradient_exponents == exponent, jnp.float32(2.0**exponent), jnp.float32(0.0)
        )
    return scaling


def expand_grad(gradient_mantissas, gradient_exponents):
    blocks = gradient_exponents.shape[1]
    scaling = block_scale(gradient_exponents)
    widened = (
        gradient_mantissas.astype(jnp.float32).reshape(gradient_mantissas.shape[0], blocks, -1)
        * scaling[:, :, None]
    )
    return widened.reshape(gradient_mantissas.shape).astype(jnp.bfloat16)


def slot_table(route_block, experts, capacity):
    flat_routes = route_block.reshape(-1)
    onehot = (flat_routes[:, None] == jnp.arange(experts, dtype=jnp.int32)[None, :]).astype(
        jnp.int32
    )
    running = jnp.cumsum(onehot, axis=0) - 1
    slot_index = jnp.sum(running * onehot, axis=1)
    return flat_routes * capacity + slot_index


def reduced_projection(current_row_block, adapter_second_factor):
    return lax.dot_general(
        current_row_block,
        adapter_second_factor,
        (((1,), (1,)), ((), ())),
        preferred_element_type=jnp.float32,
    ).astype(jnp.bfloat16)


def per_expert_terms(
    current_row_block,
    routing_share,
    reduced_input,
    stored_rows,
    expert_down_matrix,
    adapter_first_factor,
    expert_gate_value,
):
    contract_dimensions = (((1,), (1,)), ((), ()))
    base_term = lax.dot_general(
        current_row_block,
        expert_down_matrix,
        contract_dimensions,
        preferred_element_type=jnp.float32,
    )
    adapter_side_term = lax.dot_general(
        reduced_input, adapter_first_factor, contract_dimensions, preferred_element_type=jnp.float32
    )
    combined = base_term + expert_gate_value * adapter_side_term
    share_col = routing_share.astype(jnp.float32)[:, None]
    hidden_gradient = (share_col * combined).astype(jnp.bfloat16)
    weight_grad = jnp.sum(stored_rows.astype(jnp.float32) * combined, axis=1)
    low_float = reduced_input.astype(jnp.float32)
    rows_dims = (((0,), (0,)), ((), ()))
    pushed = (expert_gate_value * share_col * low_float).astype(jnp.bfloat16)
    a_grad = lax.dot_general(stored_rows, pushed, rows_dims, preferred_element_type=jnp.float32)
    reduced_rank_rows = jnp.dot(
        stored_rows, adapter_first_factor, preferred_element_type=jnp.float32
    )
    pulled = (expert_gate_value * share_col * reduced_rank_rows).astype(jnp.bfloat16)
    b_grad = lax.dot_general(
        pulled, current_row_block, rows_dims, preferred_element_type=jnp.float32
    )
    gate_term = jnp.sum(
        routing_share.astype(jnp.float32) * jnp.sum(reduced_rank_rows * low_float, axis=1)
    )
    return (hidden_gradient, weight_grad, a_grad, b_grad, gate_term)


def body(
    gradient_mantissas,
    gradient_exponents,
    routes,
    routing_weight,
    stored_hidden_rows,
    frozen_down_weight,
    adapter_first_factor,
    adapter_second_factor,
    expert_adapter_gate,
):
    experts = expert_adapter_gate.shape[0]
    sources = stored_hidden_rows.shape[1]
    capacity = stored_hidden_rows.shape[2]
    hidden_width = stored_hidden_rows.shape[3]
    tok_count, top_count = routes.shape
    slots_all = experts * capacity
    grad_out = expand_grad(gradient_mantissas, gradient_exponents)
    dest = slot_table(routes, experts, capacity)
    token_ids = jnp.arange(tok_count * top_count, dtype=jnp.int32) // top_count
    token_of = jnp.zeros((slots_all,), jnp.int32).at[dest].set(token_ids)
    share_send = (
        jnp.zeros((slots_all,), jnp.bfloat16)
        .at[dest]
        .set(routing_weight.reshape(-1))
        .reshape(experts, capacity)
    )
    row_send = grad_out[token_of].reshape(experts, capacity, -1)
    received_rows = sources * capacity
    token_low = reduced_projection(grad_out, adapter_second_factor)
    low_send = token_low[token_of].reshape(experts, capacity, -1)
    row_recv, share_recv, low_recv = (
        lax.all_to_all(row_send, "ex", split_axis=0, concat_axis=0, tiled=True),
        lax.all_to_all(share_send, "ex", split_axis=0, concat_axis=0, tiled=True),
        lax.all_to_all(low_send, "ex", split_axis=0, concat_axis=0, tiled=True),
    )
    current_row_block = row_recv.reshape(received_rows, -1)
    reduced_input = low_recv.reshape(received_rows, -1)
    routing_share = share_recv.reshape(received_rows)
    stored_rows = stored_hidden_rows.reshape(received_rows, hidden_width)
    expert_down_matrix = frozen_down_weight[0]
    own_index = lax.axis_index("ex")
    expert_gate_value = lax.dynamic_index_in_dim(expert_adapter_gate, own_index, 0, keepdims=False)
    hidden_gradient, weight_grad, a_grad, b_grad, gate_term = per_expert_terms(
        current_row_block,
        routing_share,
        reduced_input,
        stored_rows,
        expert_down_matrix,
        adapter_first_factor,
        expert_gate_value,
    )
    returned = lax.all_to_all(
        weight_grad.reshape(sources, capacity), "ex", split_axis=0, concat_axis=0, tiled=True
    )
    routing_gradient = returned.reshape(-1)[dest].reshape(tok_count, top_count)
    own_gate = (jnp.arange(experts, dtype=jnp.int32) == own_index).astype(jnp.float32) * gate_term
    a_total, b_total, gate_total = lax.psum((a_grad, b_grad, own_gate), "ex")
    hidden_out = hidden_gradient.reshape(1, sources, capacity, hidden_width)
    return (hidden_out, routing_gradient, a_total, b_total, gate_total)


def solution(mesh):
    return jax.shard_map(
        small_body if mesh.shape["ex"] == 16 else body,
        mesh=mesh,
        in_specs=(
            P(("groups", "ex"), None),
            P(("groups", "ex"), None),
            P(("groups", "ex"), None),
            P(("groups", "ex"), None),
            P(("groups", "ex"), None, None, None),
            P("ex", None, None),
            P(),
            P(),
            P(),
        ),
        out_specs=(
            P(("groups", "ex"), None, None, None),
            P(("groups", "ex"), None),
            P("groups", None),
            P("groups", None),
            P("groups"),
        ),
        check_vma=False,
    )
```

```python
import functools

import jax
import jax.numpy as jnp
from jax import lax
from jax.experimental import pallas as pl
from jax.experimental.pallas import tpu as pltpu
from jax.sharding import PartitionSpec as P

F32, BF16 = jnp.float32, jnp.bfloat16
VMEM_LIMIT = 16 * 1024 * 1024
BIG_LIMIT = 59 * 1024 * 1024
TILE, AHEAD = 384, 2
ROWS = (((0,), (0,)), ((), ()))
LANES = (((1,), (1,)), ((), ()))
PLAIN = (((1,), (0,)), ((), ()))


def dot(a, b, dims):
    return lax.dot_general(a, b, dims, preferred_element_type=F32)


SMALL = pl.CostEstimate(flops=1000000, bytes_accessed=10000, transcendentals=0)

LARGE = pl.CostEstimate(flops=30000000000, bytes_accessed=10000, transcendentals=0)


def params(limit=VMEM_LIMIT):
    return pltpu.CompilerParams(vmem_limit_bytes=limit)


def whole(count):
    return [pl.BlockSpec(memory_space=pltpu.VMEM)] * count


def scale_kernel(mantissa_ref, exponent_ref, rows_ref):
    exponents = exponent_ref[...]
    scale = jnp.zeros(exponents.shape, F32)
    for power in range(-2, 3):
        scale = scale + jnp.where(exponents == power, F32(2.0**power), F32(0.0))
    columns = scale.T
    width = mantissa_ref.shape[1] // exponents.shape[0]
    for block in range(exponents.shape[0]):
        lanes = slice(block * width, (block + 1) * width)
        rows_ref[:, lanes] = (mantissa_ref[:, lanes].astype(F32) * columns[:, block : block + 1]).astype(BF16)


def share_table(routes, weights, experts):
    expert = lax.broadcasted_iota(jnp.int32, (experts, routes.shape[1]), 0)
    table = jnp.zeros(expert.shape, F32)
    for k in range(routes.shape[0]):
        table = table + jnp.where(routes[k : k + 1] == expert, weights[k : k + 1], F32(0.0))
    return table


def pack_kernel(
    own_ref, rows_ref, second_ref, routes_ref, weights_ref, stored_ref, first_ref, gate_ref, out_ref
):
    devices, cap = stored_ref.shape[0], stored_ref.shape[1]
    rank = second_ref.shape[0]
    gate = gate_ref[own_ref[0]]
    reduced = dot(second_ref[...], rows_ref[...], LANES).astype(BF16)
    table = share_table(routes_ref[...], weights_ref[...].astype(F32), devices).astype(BF16)
    first = first_ref[...]
    pad = jnp.zeros((rank, out_ref.shape[2] - cap), BF16)
    for peer in range(devices):
        out_ref[peer, 0:rank, :] = reduced
        pulled = (gate * dot(first, stored_ref[peer], LANES)).astype(BF16)
        out_ref[peer, rank : 2 * rank, :] = jnp.concatenate([pulled, pad], axis=1)
        out_ref[peer, 2 * rank :, :] = table


def slot_of(table):
    tokens = table.shape[1]
    earlier = lax.broadcasted_iota(jnp.int32, (tokens, tokens), 0) < lax.broadcasted_iota(
        jnp.int32, (tokens, tokens), 1
    )
    taken = jnp.where(table > 0, F32(1.0), F32(0.0)).astype(BF16)
    count = dot(taken, jnp.where(earlier, F32(1.0), F32(0.0)).astype(BF16), PLAIN)
    return jnp.where(table > 0, count, F32(-1.0)).astype(jnp.int32)


def take_row(table, row):
    rows = lax.broadcasted_iota(jnp.int32, table.shape, 0)
    return jnp.sum(jnp.where(rows == row, table, F32(0.0)), axis=0, keepdims=True)


def chunk_of(j, own, devices):
    half = devices // 2
    return 2 * j + (own & 1) if j < half else 2 * (j - half) + ((own & 1) ^ 1)


def low_rank_kernel(
    own_ref,
    got_ref,
    stored_ref,
    first_ref,
    gate_ref,
    routes_ref,
    weights_ref,
    rows_ref,
    out_ref,
    wide_ref,
    narrow_ref,
):
    devices, cap = stored_ref.shape[0], stored_ref.shape[1]
    own = own_ref[0]
    rank = first_ref.shape[0]
    tokens = got_ref.shape[2]
    gate = gate_ref[own]
    shares = jnp.concatenate(
        [take_row(got_ref[s, 2 * rank :, :].astype(F32), own) for s in range(devices)], axis=0
    )
    slots = slot_of(shares)
    place = lax.broadcasted_iota(jnp.int32, (tokens, tokens), 0)
    total = jnp.zeros((rank, stored_ref.shape[2]), F32)
    for s in range(devices):
        chosen = jnp.where(place == slots[s : s + 1], F32(1.0), F32(0.0)).astype(BF16)
        pushed = (got_ref[s, 0:rank, :].astype(F32) * shares[s : s + 1]).astype(BF16)
        by_slot = dot(pushed, chosen[:cap], LANES).astype(BF16)
        total = total + dot(by_slot, stored_ref[s], PLAIN)
    gate_term = jnp.sum(total * first_ref[...].astype(F32))
    total = gate * total
    narrow_ref[...] = jnp.zeros(narrow_ref.shape, F32)
    for i in range(2 * (total.shape[1] // 128)):
        narrow_ref[i] = total[(i % 2) * 16 : (i % 2) * 16 + 16, (i // 2) * 128 : (i // 2) * 128 + 128]
    lane = lax.broadcasted_iota(jnp.int32, (16, 128), 1)
    row = lax.broadcasted_iota(jnp.int32, (16, 128), 0)
    narrow_ref[devices - 1] = jnp.where((lane == own) & (row == 0), gate_term, F32(0.0))

    table = share_table(routes_ref[...], weights_ref[...].astype(F32), devices)
    mine = slot_of(table)
    pulled = jnp.zeros((rank, tokens), F32)
    for e in range(devices):
        weighted = jnp.where(place == mine[e : e + 1], table[e : e + 1], F32(0.0)).astype(BF16)
        pulled = pulled + dot(got_ref[e, rank : 2 * rank, :], weighted, PLAIN)
    coarse = pulled.astype(BF16)
    fine = (pulled - coarse.astype(F32)).astype(BF16)
    both = jnp.concatenate([coarse, fine], axis=0)
    result = dot(both, rows_ref[...], PLAIN)
    wide_ref[...] = result[:rank] + result[rank:]
    columns = wide_ref.shape[1] // devices
    for j in range(devices):
        chunk = chunk_of(j, own, devices)
        for b in range(columns // 128):
            lanes = pl.ds(pl.multiple_of(chunk * columns + b * 128, 128), 128)
            out_ref[j, b * rank : (b + 1) * rank, :] = wide_ref[:, lanes]
        out_ref[j, 64:80, :] = narrow_ref[chunk]


def unpack_kernel(own_ref, got_ref, second_ref, first_ref, gate_ref, narrow_ref):
    devices = got_ref.shape[0]
    own = own_ref[0]
    rank = second_ref.shape[0]
    columns = second_ref.shape[1] // devices
    for j in range(devices):
        chunk = chunk_of(j, own, devices)
        for b in range(columns // 128):
            lanes = pl.ds(pl.multiple_of(chunk * columns + b * 128, 128), 128)
            second_ref[:, lanes] = got_ref[j, b * rank : (b + 1) * rank, :].astype(F32)
        narrow_ref[chunk] = got_ref[j, 64:80, :].astype(F32)
    for i in range(2 * (first_ref.shape[1] // 128)):
        first_ref[(i % 2) * 16 : (i % 2) * 16 + 16, (i // 2) * 128 : (i // 2) * 128 + 128] = narrow_ref[i]
    gate_ref[...] = narrow_ref[devices - 1][0:8]


def expert_kernel(
    place_ref,
    gate_ref,
    weight_ref,
    other_weight_ref,
    stored_ref,
    other_stored_ref,
    first_ref,
    got_ref,
    *rest,
    layout,
    slot,
):
    hidden_out, other_out, dots_out, mark_ref, rows_ref, held_ref, kept_ref, hidden_ref, dots_ref = rest[-17:-8]
    adapted_ref, chosen_ref, shares_ref, results_ref, load_sem, held_sem, kept_sem, write_sem = rest[-8:]
    tile = held_ref.shape[1]
    tiles = weight_ref.shape[1] // tile
    own, is_end = place_ref[0], place_ref[1]
    cap = stored_ref.shape[1]
    rank = first_ref.shape[0]
    units = len(layout)
    tokens = rows_ref.shape[0] // units
    choices, taken = ([], []), 0
    for unit, counts in enumerate(layout):
        for role, count in enumerate(counts):
            begin = unit * tokens
            for k in range(count):
                piece = rest[taken]
                target = rows_ref.at[begin : begin + piece.shape[0]]
                choices[role].append(pltpu.make_async_copy(piece, target, load_sem.at[len(choices[role])]))
                begin += piece.shape[0]
                taken += 1
    for flag, copies in ((1, choices[0]), (0, choices[1])):

        @pl.when(is_end == flag)
        def _():
            for copy in copies:
                copy.start()

    kept = []
    for k, stored in enumerate((stored_ref, other_stored_ref)):
        for unit in range(units):
            kept.append(
                pltpu.make_async_copy(
                    stored.at[place_ref[2 + unit]], kept_ref.at[k, unit], kept_sem.at[k * units + unit]
                )
            )
            kept[-1].start()

    def load(n):
        begin = pl.multiple_of(n % tiles * tile, tile)
        at = lambda weight: pltpu.make_async_copy(weight.at[0, pl.ds(begin, tile)], held_ref.at[n], held_sem.at[n])

        @pl.when(n < tiles)
        def _():
            at(weight_ref).start()

        @pl.when(n >= tiles)
        def _():
            at(other_weight_ref).start()

    for n in range(AHEAD):
        load(jnp.int32(n))

    place = lax.broadcasted_iota(jnp.int32, (cap, tokens), 0)
    for unit in range(units):
        source = place_ref[2 + unit]
        table = got_ref[source, 2 * rank :, :].astype(F32)
        shares = jnp.concatenate(
            [take_row(table, own), take_row(table, own ^ 1), jnp.zeros((6, tokens), F32)], axis=0
        )
        slots = slot_of(shares)
        columns = shares.T
        adapted_ref[unit] = dot(got_ref[source, 0:rank, :], first_ref[...], ROWS)
        for k in range(2):
            chosen_ref[k, unit] = jnp.where(place == slots[k : k + 1], F32(1.0), F32(0.0)).astype(BF16)
            shares_ref[k, unit] = jnp.broadcast_to(columns[:, k : k + 1], (tokens, 128))
    results_ref[...] = jnp.zeros(results_ref.shape, F32)
    for copy in kept:
        copy.wait()
    for flag, copies in ((1, choices[0]), (0, choices[1])):

        @pl.when(is_end == flag)
        def _():
            for copy in copies:
                copy.wait()

    lane = lax.broadcasted_iota(jnp.int32, (tokens, 128), 1)

    @pl.loop(0, 2 * tiles)
    def _(n):
        @pl.when(n + AHEAD < 2 * tiles)
        def _():
            load(n + AHEAD)

        k = n // tiles
        span = pl.ds(pl.multiple_of(n % tiles * tile, tile), tile)
        pltpu.make_async_copy(weight_ref.at[0, 0:tile], held_ref.at[n], held_sem.at[n]).wait()
        grads = dot(rows_ref[...], held_ref[n], LANES)
        gate = gate_ref[own ^ k]
        for unit in range(units):
            chosen = chosen_ref[k, unit]
            by_token = dot(chosen, kept_ref[k, unit, :, span], ROWS)
            grad = grads[unit * tokens : (unit + 1) * tokens] + gate * adapted_ref[unit, :, span]
            partial = jnp.sum(by_token * grad, axis=1, keepdims=True)
            results_ref[unit] += jnp.where(lane == k, partial, F32(0.0))
            shared = dot(chosen, (shares_ref[k, unit, :, 0:1] * grad).astype(BF16), PLAIN)
            hidden_ref[k, unit, :, span] = shared.astype(BF16)

    for unit in range(units):
        dots_ref[unit] = results_ref[unit].T[:8]
    writes = []
    for unit in range(units):
        source = place_ref[2 + unit]
        for value, target in (
            (dots_ref.at[unit], dots_out.at[source >> 1]),
            (hidden_ref.at[0, unit], hidden_out.at[source]),
            (hidden_ref.at[1, unit], other_out.at[slot + unit]),
        ):
            writes.append(pltpu.make_async_copy(value, target, write_sem.at[len(writes)]))
            writes[-1].start()
    mark_ref[...] = jnp.zeros(mark_ref.shape, F32)
    for copy in writes:
        copy.wait()


def expert_call(place, gate, weight, other_weight, stored, other_stored, first, got, buffers, hidden, other, dots, mark, slot):
    devices, cap, width_hidden = stored.shape
    layout = [(len(as_end), len(as_mid)) for as_end, as_mid in buffers]
    pieces = [piece for pair in buffers for side in pair for piece in side]
    width = pieces[0].shape[1]
    tokens = got.shape[2]
    units = len(buffers)
    any_spec = pl.BlockSpec(memory_space=pl.ANY)
    smem = pl.BlockSpec(memory_space=pltpu.SMEM)
    operands = [place, gate, weight, other_weight, stored, other_stored, first, got, *pieces]
    in_specs = [smem] * 2 + [any_spec] * 4 + whole(2) + [any_spec] * len(pieces)
    if mark is not None:
        operands.append(mark)
        in_specs.append(any_spec)
    aliases, sizes = {}, []
    for number, value in enumerate((hidden, other, dots)):
        if isinstance(value, int):
            sizes.append(value)
        else:
            sizes.append(value.shape[0])
            aliases[len(operands)] = number
            operands.append(value)
            in_specs.append(any_spec)
    loads = max(sum(counts[role] for counts in layout) for role in range(2))
    return pl.pallas_call(
        functools.partial(expert_kernel, layout=layout, slot=slot),
        in_specs=in_specs,
        out_specs=[any_spec, any_spec, any_spec, pl.BlockSpec(memory_space=pltpu.VMEM)],
        out_shape=[
            jax.ShapeDtypeStruct((sizes[0], cap, width_hidden), BF16),
            jax.ShapeDtypeStruct((sizes[1], cap, width_hidden), BF16),
            jax.ShapeDtypeStruct((sizes[2], 8, tokens), F32),
            jax.ShapeDtypeStruct((8, 128), F32),
        ],
        scratch_shapes=[
            pltpu.VMEM((units * tokens, width), BF16),
            pltpu.VMEM((2 * width_hidden // TILE, TILE, width), BF16),
            pltpu.VMEM((2, units, cap, width_hidden), BF16),
            pltpu.VMEM((2, units, cap, width_hidden), BF16),
            pltpu.VMEM((units, 8, tokens), F32),
            pltpu.VMEM((units, tokens, width_hidden), F32),
            pltpu.VMEM((2, units, cap, tokens), BF16),
            pltpu.VMEM((2, units, tokens, 128), F32),
            pltpu.VMEM((units, tokens, 128), F32),
            pltpu.SemaphoreType.DMA((loads,)),
            pltpu.SemaphoreType.DMA((2 * width_hidden // TILE,)),
            pltpu.SemaphoreType.DMA((2 * units,)),
            pltpu.SemaphoreType.DMA((3 * units,)),
        ],
        input_output_aliases=aliases,
        compiler_params=params(BIG_LIMIT),
        cost_estimate=SMALL,
    )(*operands)


def place_kernel(own_ref, *refs, masks):
    hidden_ref, sem = refs[-2:]
    copies = []
    for moved_ref, turns in zip(refs, masks):
        for k, mask in enumerate(turns):
            source = own_ref[0] ^ 1 ^ (mask << 1)
            copies.append(pltpu.make_async_copy(moved_ref.at[k], hidden_ref.at[source], sem.at[len(copies)]))
    for copy in copies:
        copy.start()
    for copy in copies:
        copy.wait()


def place_call(own1, moved, hidden, masks):
    any_spec = pl.BlockSpec(memory_space=pl.ANY)
    return pl.pallas_call(
        functools.partial(place_kernel, masks=masks),
        in_specs=[pl.BlockSpec(memory_space=pltpu.SMEM)] + whole(len(moved)) + [any_spec],
        out_specs=any_spec,
        out_shape=jax.ShapeDtypeStruct(hidden.shape, hidden.dtype),
        input_output_aliases={1 + len(moved): 0},
        scratch_shapes=[pltpu.SemaphoreType.DMA((sum(len(turns) for turns in masks),))],
        compiler_params=params(),
        cost_estimate=SMALL,
    )(own1, *moved, hidden)


def finish_kernel(own_ref, dots_ref, routes_ref, moved_ref, _, __, routing_ref, hidden_ref, sem, *, mask):
    own = own_ref[0]
    copy = pltpu.make_async_copy(moved_ref.at[0], hidden_ref.at[own ^ 1 ^ (mask << 1)], sem)
    copy.start()
    routes = routes_ref[...]
    total = jnp.zeros(routes.shape, F32)
    for chip in range(dots_ref.shape[0]):
        for row in range(2):
            expert = 2 * chip + ((own & 1) ^ row)
            total = total + jnp.where(routes == expert, dots_ref[chip, row : row + 1, :], F32(0.0))
    routing_ref[...] = total
    copy.wait()


def permutes():
    number = lambda z, x, c: (z * 2 + x) * 2 + c
    places = [(z, x, c) for z in range(4) for x in range(2) for c in range(2)]
    end = lambda z: z in (0, 3)
    return dict(
        near=[(number(z, x, c), number(z ^ 1, x, c)) for z, x, c in places],
        mid=[(number(z, x, c), number(3 - z, x, c)) for z, x, c in places if not end(z)],
        out=[(number(z, x, c), number(z ^ 1, x, c)) for z, x, c in places if not end(z)],
        side=[(number(z, x, c), number(z, 1 - x, c)) for z, x, c in places],
        end_side=[(number(z, x, c), number(z, 1 - x, c)) for z, x, c in places if end(z)],
    )


def xor_pairs(mask):
    return [(i, i ^ mask) for i in range(16)]


def send(value, pairs):
    return lax.ppermute(value, "ex", pairs)


def then(value, *earlier):
    return lax.optimization_barrier((value, *earlier))[0]


def small_body(
    gradient_mantissas,
    gradient_exponents,
    routes,
    routing_weight,
    stored_hidden_rows,
    frozen_down_weight,
    adapter_first_factor,
    adapter_second_factor,
    expert_adapter_gate,
):
    tokens, width = gradient_mantissas.shape
    stored = stored_hidden_rows[0]
    devices, cap, hidden = stored.shape
    rank = adapter_second_factor.shape[0]
    first = adapter_first_factor.T
    routes_t, weights_t = routes.T, routing_weight.T
    own = lax.axis_index("ex").astype(jnp.int32)
    own1 = own.reshape(1)
    z = own >> 2
    is_end = ((z == 0) | (z == 3)).astype(jnp.int32)

    smem = pl.BlockSpec(memory_space=pltpu.SMEM)
    vmem = pl.BlockSpec(memory_space=pltpu.VMEM)
    any_spec = pl.BlockSpec(memory_space=pl.ANY)
    to = permutes()
    pick = lambda as_end, as_mid: jnp.where(is_end == 1, as_end, as_mid)

    smem = pl.BlockSpec(memory_space=pltpu.SMEM)
    vmem = pl.BlockSpec(memory_space=pltpu.VMEM)
    any_spec = pl.BlockSpec(memory_space=pl.ANY)
    to = permutes()
    pick = lambda as_end, as_mid: jnp.where(is_end == 1, as_end, as_mid)

    other_weight = send(frozen_down_weight, xor_pairs(1))
    other_stored = send(stored, xor_pairs(1))
    rows = pl.pallas_call(
        scale_kernel,
        in_specs=whole(2),
        out_specs=vmem,
        out_shape=jax.ShapeDtypeStruct((tokens, width), BF16),
        compiler_params=params(),
        cost_estimate=SMALL,
    )(gradient_mantissas, gradient_exponents.T)
    masks = (0, 2, 1, 4, 3, 6, 5, 7)
    final = len(masks) - 1
    half = tokens // 2
    hidden_part, other_part, dots, mark, begin = devices, 5, devices // 2, None, 0

    def experts(count, buffers, *earlier):
        nonlocal hidden_part, other_part, dots, mark, begin
        turns = masks[begin : begin + count]
        place = jnp.stack([own, is_end] + [own ^ (mask << 1) for mask in turns])
        hidden_part, other_part, dots, mark = expert_call(
            then(place, *earlier),
            expert_adapter_gate,
            frozen_down_weight,
            other_weight,
            stored,
            other_stored,
            first,
            got,
            buffers,
            hidden_part,
            other_part,
            dots,
            mark,
            begin if begin < 5 else 0,
        )
        begin += count
        return mark

    near, side, mid = send(rows, to["near"]), send(rows, to["side"]), send(rows, to["mid"])
    packed = pl.pallas_call(
        pack_kernel,
        in_specs=[smem] + whole(6) + [smem],
        out_specs=vmem,
        out_shape=jax.ShapeDtypeStruct((devices, 2 * rank + devices, tokens), BF16),
        compiler_params=params(),
        cost_estimate=SMALL,
    )(
        then(own1, other_stored),
        rows,
        adapter_second_factor,
        routes_t,
        weights_t,
        stored,
        first,
        expert_adapter_gate,
    )
    got = lax.all_to_all(packed, "ex", split_axis=0, concat_axis=0, tiled=True)
    near, side, mid, _, _ = lax.optimization_barrier((near, side, mid, got, other_weight))
    near2 = send(pick(side, mid), to["near"])
    side2 = send(pick(near, mid), to["side"])
    mid2 = send(near, to["mid"])
    partial = pl.pallas_call(
        low_rank_kernel,
        in_specs=[smem] + whole(3) + [smem] + whole(3),
        out_specs=vmem,
        out_shape=jax.ShapeDtypeStruct((devices, 80, 128), F32),
        scratch_shapes=[pltpu.VMEM((rank, width), F32), pltpu.VMEM((devices, 16, 128), F32)],
        compiler_params=params(),
        cost_estimate=SMALL,
    )(then(own1, near, side, mid), got, stored, first, expert_adapter_gate, routes_t, weights_t, rows)
    lanes = [[2 * chip + core for chip in range(devices // 2)] for core in range(2)]
    among_lane = lambda value: lax.all_to_all(
        value, "ex", split_axis=0, concat_axis=0, axis_index_groups=lanes, tiled=True
    )
    pair = (partial[: devices // 2] + send(partial[devices // 2 :], xor_pairs(1))).astype(BF16)
    parts = among_lane(pair)
    found = experts(1, [([rows], [rows])], pair, near, side, mid)
    near2, mid2, side2, parts, _ = lax.optimization_barrier((near2, mid2, side2, parts, found))
    near3 = send(mid2, to["out"])
    side3 = send(pick(near2, mid2), to["side"])
    summed = jnp.sum(parts.astype(F32), axis=0).astype(BF16)
    summed = among_lane(jnp.broadcast_to(summed[None], (devices // 2, 80, 128)))
    found = experts(4, [([near], [near]), ([side], [side]), ([near2], [mid2]), ([side2], [near2])], near2, side2, mid2)
    near3, side3, summed, _ = lax.optimization_barrier((near3, side3, summed, found))
    last = [send(near3[:half], to["end_side"]), send(side3[half:], to["out"])]
    moved, other_part = [send(then(other_part, near3, side3), xor_pairs(1))], 2
    found = experts(2, [([near3], [mid]), ([side3], [side3])], near3, side3, moved[0])
    summed = then(summed, found)
    summed = jnp.concatenate([summed, send(summed, xor_pairs(1))], axis=0)
    moved.append(send(other_part, xor_pairs(1)))
    other_part = 1
    found = experts(1, [(last, [side2])], *last)
    last_moved = send(other_part, xor_pairs(1))
    second_grad, first_grad, gate_grad = pl.pallas_call(
        unpack_kernel,
        in_specs=[smem] + whole(1),
        out_specs=whole(3),
        out_shape=[
            jax.ShapeDtypeStruct((rank, width), F32),
            jax.ShapeDtypeStruct((rank, hidden), F32),
            jax.ShapeDtypeStruct((8, 128), F32),
        ],
        scratch_shapes=[pltpu.VMEM((devices, 16, 128), F32)],
        compiler_params=params(),
        cost_estimate=SMALL,
    )(then(own1, found), summed)
    hidden_part = place_call(own1, moved, hidden_part, (masks[:5], masks[5:final]))
    moved = last_moved
    returned = among_lane(dots)
    routing_t, hidden_gradient = pl.pallas_call(
        functools.partial(finish_kernel, mask=masks[-1]),
        in_specs=[smem] + whole(3) + [any_spec, any_spec],
        out_specs=[vmem, any_spec],
        out_shape=[
            jax.ShapeDtypeStruct(routes_t.shape, F32),
            jax.ShapeDtypeStruct((devices, cap, hidden), BF16),
        ],
        input_output_aliases={4: 1},
        scratch_shapes=[pltpu.SemaphoreType.DMA],
        compiler_params=params(),
        cost_estimate=SMALL,
    )(own1, returned, routes_t, moved, hidden_part, mark)
    return (
        hidden_gradient[None],
        routing_t.T,
        first_grad.T,
        second_grad,
        gate_grad[0, :devices],
    )


def block_scale(gradient_exponents):
    scaling = jnp.zeros(gradient_exponents.shape, jnp.float32)
    for exponent in range(-2, 3):
        scaling = scaling + jnp.where(
            gradient_exponents == exponent, jnp.float32(2.0**exponent), jnp.float32(0.0)
        )
    return scaling


def expand_grad(gradient_mantissas, gradient_exponents):
    blocks = gradient_exponents.shape[1]
    scaling = block_scale(gradient_exponents)
    widened = (
        gradient_mantissas.astype(jnp.float32).reshape(gradient_mantissas.shape[0], blocks, -1)
        * scaling[:, :, None]
    )
    return widened.reshape(gradient_mantissas.shape).astype(jnp.bfloat16)


def slot_table(route_block, experts, capacity):
    flat_routes = route_block.reshape(-1)
    onehot = (flat_routes[:, None] == jnp.arange(experts, dtype=jnp.int32)[None, :]).astype(
        jnp.int32
    )
    running = jnp.cumsum(onehot, axis=0) - 1
    slot_index = jnp.sum(running * onehot, axis=1)
    return flat_routes * capacity + slot_index


def reduced_projection(current_row_block, adapter_second_factor):
    return lax.dot_general(
        current_row_block,
        adapter_second_factor,
        (((1,), (1,)), ((), ())),
        preferred_element_type=jnp.float32,
    ).astype(jnp.bfloat16)


def per_expert_terms(
    current_row_block,
    routing_share,
    reduced_input,
    stored_rows,
    expert_down_matrix,
    adapter_first_factor,
    expert_gate_value,
):
    contract_dimensions = (((1,), (1,)), ((), ()))
    base_term = lax.dot_general(
        current_row_block,
        expert_down_matrix,
        contract_dimensions,
        preferred_element_type=jnp.float32,
    )
    adapter_side_term = lax.dot_general(
        reduced_input, adapter_first_factor, contract_dimensions, preferred_element_type=jnp.float32
    )
    combined = base_term + expert_gate_value * adapter_side_term
    share_col = routing_share.astype(jnp.float32)[:, None]
    hidden_gradient = (share_col * combined).astype(jnp.bfloat16)
    weight_grad = jnp.sum(stored_rows.astype(jnp.float32) * combined, axis=1)
    low_float = reduced_input.astype(jnp.float32)
    rows_dims = (((0,), (0,)), ((), ()))
    pushed = (expert_gate_value * share_col * low_float).astype(jnp.bfloat16)
    a_grad = lax.dot_general(stored_rows, pushed, rows_dims, preferred_element_type=jnp.float32)
    reduced_rank_rows = jnp.dot(
        stored_rows, adapter_first_factor, preferred_element_type=jnp.float32
    )
    pulled = (expert_gate_value * share_col * reduced_rank_rows).astype(jnp.bfloat16)
    b_grad = lax.dot_general(
        pulled, current_row_block, rows_dims, preferred_element_type=jnp.float32
    )
    gate_term = jnp.sum(
        routing_share.astype(jnp.float32) * jnp.sum(reduced_rank_rows * low_float, axis=1)
    )
    return (hidden_gradient, weight_grad, a_grad, b_grad, gate_term)


def body(
    gradient_mantissas,
    gradient_exponents,
    routes,
    routing_weight,
    stored_hidden_rows,
    frozen_down_weight,
    adapter_first_factor,
    adapter_second_factor,
    expert_adapter_gate,
):
    experts = expert_adapter_gate.shape[0]
    sources = stored_hidden_rows.shape[1]
    capacity = stored_hidden_rows.shape[2]
    hidden_width = stored_hidden_rows.shape[3]
    tok_count, top_count = routes.shape
    slots_all = experts * capacity
    grad_out = expand_grad(gradient_mantissas, gradient_exponents)
    dest = slot_table(routes, experts, capacity)
    token_ids = jnp.arange(tok_count * top_count, dtype=jnp.int32) // top_count
    token_of = jnp.zeros((slots_all,), jnp.int32).at[dest].set(token_ids)
    share_send = (
        jnp.zeros((slots_all,), jnp.bfloat16)
        .at[dest]
        .set(routing_weight.reshape(-1))
        .reshape(experts, capacity)
    )
    row_send = grad_out[token_of].reshape(experts, capacity, -1)
    received_rows = sources * capacity
    token_low = reduced_projection(grad_out, adapter_second_factor)
    low_send = token_low[token_of].reshape(experts, capacity, -1)
    row_recv, share_recv, low_recv = (
        lax.all_to_all(row_send, "ex", split_axis=0, concat_axis=0, tiled=True),
        lax.all_to_all(share_send, "ex", split_axis=0, concat_axis=0, tiled=True),
        lax.all_to_all(low_send, "ex", split_axis=0, concat_axis=0, tiled=True),
    )
    current_row_block = row_recv.reshape(received_rows, -1)
    reduced_input = low_recv.reshape(received_rows, -1)
    routing_share = share_recv.reshape(received_rows)
    stored_rows = stored_hidden_rows.reshape(received_rows, hidden_width)
    expert_down_matrix = frozen_down_weight[0]
    own_index = lax.axis_index("ex")
    expert_gate_value = lax.dynamic_index_in_dim(expert_adapter_gate, own_index, 0, keepdims=False)
    hidden_gradient, weight_grad, a_grad, b_grad, gate_term = per_expert_terms(
        current_row_block,
        routing_share,
        reduced_input,
        stored_rows,
        expert_down_matrix,
        adapter_first_factor,
        expert_gate_value,
    )
    returned = lax.all_to_all(
        weight_grad.reshape(sources, capacity), "ex", split_axis=0, concat_axis=0, tiled=True
    )
    routing_gradient = returned.reshape(-1)[dest].reshape(tok_count, top_count)
    own_gate = (jnp.arange(experts, dtype=jnp.int32) == own_index).astype(jnp.float32) * gate_term
    a_total, b_total, gate_total = lax.psum((a_grad, b_grad, own_gate), "ex")
    hidden_out = hidden_gradient.reshape(1, sources, capacity, hidden_width)
    return (hidden_out, routing_gradient, a_total, b_total, gate_total)


def solution(mesh):
    return jax.shard_map(
        small_body if mesh.shape["ex"] == 16 else body,
        mesh=mesh,
        in_specs=(
            P(("groups", "ex"), None),
            P(("groups", "ex"), None),
            P(("groups", "ex"), None),
            P(("groups", "ex"), None),
            P(("groups", "ex"), None, None, None),
            P("ex", None, None),
            P(),
            P(),
            P(),
        ),
        out_specs=(
            P(("groups", "ex"), None, None, None),
            P(("groups", "ex"), None),
            P("groups", None),
            P("groups", None),
            P("groups"),
        ),
        check_vma=False,
    )
```

```python
import functools

import jax
import jax.numpy as jnp
from jax import lax
from jax.experimental import pallas as pl
from jax.experimental.pallas import tpu as pltpu
from jax.sharding import PartitionSpec as P

F32, BF16 = jnp.float32, jnp.bfloat16
VMEM_LIMIT = 16 * 1024 * 1024
BIG_LIMIT = 59 * 1024 * 1024
TILE, AHEAD = 384, 2
ROWS = (((0,), (0,)), ((), ()))
LANES = (((1,), (1,)), ((), ()))
PLAIN = (((1,), (0,)), ((), ()))


def dot(a, b, dims):
    return lax.dot_general(a, b, dims, preferred_element_type=F32)


SMALL = pl.CostEstimate(flops=1000000, bytes_accessed=10000, transcendentals=0)

LARGE = pl.CostEstimate(flops=30000000000, bytes_accessed=10000, transcendentals=0)


def params(limit=VMEM_LIMIT):
    return pltpu.CompilerParams(vmem_limit_bytes=limit)


def whole(count):
    return [pl.BlockSpec(memory_space=pltpu.VMEM)] * count


def scale_kernel(mantissa_ref, exponent_ref, rows_ref):
    exponents = exponent_ref[...]
    scale = jnp.zeros(exponents.shape, F32)
    for power in range(-2, 3):
        scale = scale + jnp.where(exponents == power, F32(2.0**power), F32(0.0))
    columns = scale.T
    width = mantissa_ref.shape[1] // exponents.shape[0]
    for block in range(exponents.shape[0]):
        lanes = slice(block * width, (block + 1) * width)
        rows_ref[:, lanes] = (mantissa_ref[:, lanes].astype(F32) * columns[:, block : block + 1]).astype(BF16)


def share_table(routes, weights, experts):
    expert = lax.broadcasted_iota(jnp.int32, (experts, routes.shape[1]), 0)
    table = jnp.zeros(expert.shape, F32)
    for k in range(routes.shape[0]):
        table = table + jnp.where(routes[k : k + 1] == expert, weights[k : k + 1], F32(0.0))
    return table


def pack_kernel(
    own_ref, rows_ref, second_ref, routes_ref, weights_ref, stored_ref, first_ref, gate_ref, out_ref
):
    devices, cap = stored_ref.shape[0], stored_ref.shape[1]
    rank = second_ref.shape[0]
    gate = gate_ref[own_ref[0]]
    reduced = dot(second_ref[...], rows_ref[...], LANES).astype(BF16)
    table = share_table(routes_ref[...], weights_ref[...].astype(F32), devices).astype(BF16)
    first = first_ref[...]
    pad = jnp.zeros((rank, out_ref.shape[2] - cap), BF16)
    for peer in range(devices):
        out_ref[peer, 0:rank, :] = reduced
        pulled = (gate * dot(first, stored_ref[peer], LANES)).astype(BF16)
        out_ref[peer, rank : 2 * rank, :] = jnp.concatenate([pulled, pad], axis=1)
        out_ref[peer, 2 * rank :, :] = table


def slot_of(table):
    tokens = table.shape[1]
    earlier = lax.broadcasted_iota(jnp.int32, (tokens, tokens), 0) < lax.broadcasted_iota(
        jnp.int32, (tokens, tokens), 1
    )
    taken = jnp.where(table > 0, F32(1.0), F32(0.0)).astype(BF16)
    count = dot(taken, jnp.where(earlier, F32(1.0), F32(0.0)).astype(BF16), PLAIN)
    return jnp.where(table > 0, count, F32(-1.0)).astype(jnp.int32)


def take_row(table, row):
    rows = lax.broadcasted_iota(jnp.int32, table.shape, 0)
    return jnp.sum(jnp.where(rows == row, table, F32(0.0)), axis=0, keepdims=True)


def chunk_of(j, own, devices):
    half = devices // 2
    return 2 * j + (own & 1) if j < half else 2 * (j - half) + ((own & 1) ^ 1)


def low_rank_kernel(
    own_ref,
    got_ref,
    stored_ref,
    first_ref,
    gate_ref,
    routes_ref,
    weights_ref,
    rows_ref,
    out_ref,
    wide_ref,
    narrow_ref,
):
    devices, cap = stored_ref.shape[0], stored_ref.shape[1]
    own = own_ref[0]
    rank = first_ref.shape[0]
    tokens = got_ref.shape[2]
    gate = gate_ref[own]
    shares = jnp.concatenate(
        [take_row(got_ref[s, 2 * rank :, :].astype(F32), own) for s in range(devices)], axis=0
    )
    slots = slot_of(shares)
    place = lax.broadcasted_iota(jnp.int32, (tokens, tokens), 0)
    total = jnp.zeros((rank, stored_ref.shape[2]), F32)
    for s in range(devices):
        chosen = jnp.where(place == slots[s : s + 1], F32(1.0), F32(0.0)).astype(BF16)
        pushed = (got_ref[s, 0:rank, :].astype(F32) * shares[s : s + 1]).astype(BF16)
        by_slot = dot(pushed, chosen[:cap], LANES).astype(BF16)
        total = total + dot(by_slot, stored_ref[s], PLAIN)
    gate_term = jnp.sum(total * first_ref[...].astype(F32))
    total = gate * total
    narrow_ref[...] = jnp.zeros(narrow_ref.shape, F32)
    for i in range(2 * (total.shape[1] // 128)):
        narrow_ref[i] = total[(i % 2) * 16 : (i % 2) * 16 + 16, (i // 2) * 128 : (i // 2) * 128 + 128]
    lane = lax.broadcasted_iota(jnp.int32, (16, 128), 1)
    row = lax.broadcasted_iota(jnp.int32, (16, 128), 0)
    coarse_gate = jnp.full((16, 128), gate_term, F32).astype(BF16).astype(F32)
    parts = jnp.where(row == 0, coarse_gate, gate_term - coarse_gate)
    narrow_ref[devices - 1] = jnp.where((lane == own) & (row < 2), parts, F32(0.0))

    table = share_table(routes_ref[...], weights_ref[...].astype(F32), devices)
    mine = slot_of(table)
    pulled = jnp.zeros((rank, tokens), F32)
    for e in range(devices):
        weighted = jnp.where(place == mine[e : e + 1], table[e : e + 1], F32(0.0)).astype(BF16)
        pulled = pulled + dot(got_ref[e, rank : 2 * rank, :], weighted, PLAIN)
    coarse = pulled.astype(BF16)
    fine = (pulled - coarse.astype(F32)).astype(BF16)
    both = jnp.concatenate([coarse, fine], axis=0)
    result = dot(both, rows_ref[...], PLAIN)
    wide_ref[...] = result[:rank] + result[rank:]
    columns = wide_ref.shape[1] // devices
    for j in range(devices):
        chunk = chunk_of(j, own, devices)
        for b in range(columns // 128):
            lanes = pl.ds(pl.multiple_of(chunk * columns + b * 128, 128), 128)
            out_ref[j, b * rank : (b + 1) * rank, :] = wide_ref[:, lanes]
        out_ref[j, 64:80, :] = narrow_ref[chunk]


def unpack_kernel(own_ref, got_ref, second_ref, first_ref, gate_ref, narrow_ref):
    devices = got_ref.shape[0]
    own = own_ref[0]
    rank = second_ref.shape[0]
    columns = second_ref.shape[1] // devices
    for j in range(devices):
        chunk = chunk_of(j, own, devices)
        for b in range(columns // 128):
            lanes = pl.ds(pl.multiple_of(chunk * columns + b * 128, 128), 128)
            second_ref[:, lanes] = got_ref[j, b * rank : (b + 1) * rank, :].astype(F32)
        narrow_ref[chunk] = got_ref[j, 64:80, :].astype(F32)
    for i in range(2 * (first_ref.shape[1] // 128)):
        first_ref[(i % 2) * 16 : (i % 2) * 16 + 16, (i // 2) * 128 : (i // 2) * 128 + 128] = narrow_ref[i]
    gates = narrow_ref[devices - 1]
    gate_ref[...] = jnp.broadcast_to(gates[0:1] + gates[1:2], gate_ref.shape)


def expert_kernel(
    place_ref,
    gate_ref,
    weight_ref,
    other_weight_ref,
    stored_ref,
    other_stored_ref,
    first_ref,
    got_ref,
    *rest,
    layout,
    slot,
):
    hidden_out, other_out, dots_out, mark_ref, rows_ref, held_ref, kept_ref, hidden_ref, dots_ref = rest[-17:-8]
    adapted_ref, chosen_ref, shares_ref, results_ref, load_sem, held_sem, kept_sem, write_sem = rest[-8:]
    tile = held_ref.shape[1]
    tiles = weight_ref.shape[1] // tile
    own, is_end = place_ref[0], place_ref[1]
    cap = stored_ref.shape[1]
    rank = first_ref.shape[0]
    units = len(layout)
    tokens = rows_ref.shape[0] // units
    choices, taken = ([], []), 0
    for unit, counts in enumerate(layout):
        for role, count in enumerate(counts):
            begin = unit * tokens
            for k in range(count):
                piece = rest[taken]
                target = rows_ref.at[begin : begin + piece.shape[0]]
                choices[role].append(pltpu.make_async_copy(piece, target, load_sem.at[len(choices[role])]))
                begin += piece.shape[0]
                taken += 1
    for flag, copies in ((1, choices[0]), (0, choices[1])):

        @pl.when(is_end == flag)
        def _():
            for copy in copies:
                copy.start()

    kept = []
    for k, stored in enumerate((stored_ref, other_stored_ref)):
        for unit in range(units):
            kept.append(
                pltpu.make_async_copy(
                    stored.at[place_ref[2 + unit]], kept_ref.at[k, unit], kept_sem.at[k * units + unit]
                )
            )
            kept[-1].start()

    def load(n):
        begin = pl.multiple_of(n % tiles * tile, tile)
        at = lambda weight: pltpu.make_async_copy(weight.at[0, pl.ds(begin, tile)], held_ref.at[n], held_sem.at[n])

        @pl.when(n < tiles)
        def _():
            at(weight_ref).start()

        @pl.when(n >= tiles)
        def _():
            at(other_weight_ref).start()

    for n in range(AHEAD):
        load(jnp.int32(n))

    place = lax.broadcasted_iota(jnp.int32, (cap, tokens), 0)
    for unit in range(units):
        source = place_ref[2 + unit]
        table = got_ref[source, 2 * rank :, :].astype(F32)
        shares = jnp.concatenate(
            [take_row(table, own), take_row(table, own ^ 1), jnp.zeros((6, tokens), F32)], axis=0
        )
        slots = slot_of(shares)
        columns = shares.T
        adapted_ref[unit] = dot(got_ref[source, 0:rank, :], first_ref[...], ROWS)
        for k in range(2):
            chosen_ref[k, unit] = jnp.where(place == slots[k : k + 1], F32(1.0), F32(0.0)).astype(BF16)
            shares_ref[k, unit * tokens : (unit + 1) * tokens] = jnp.broadcast_to(columns[:, k : k + 1], (tokens, 128))
    results_ref[...] = jnp.zeros(results_ref.shape, F32)
    for copy in kept:
        copy.wait()
    for flag, copies in ((1, choices[0]), (0, choices[1])):

        @pl.when(is_end == flag)
        def _():
            for copy in copies:
                copy.wait()

    lane = lax.broadcasted_iota(jnp.int32, (tokens, 128), 1)

    @pl.loop(0, 2 * tiles)
    def _(n):
        @pl.when(n + AHEAD < 2 * tiles)
        def _():
            load(n + AHEAD)

        k = n // tiles
        span = pl.ds(pl.multiple_of(n % tiles * tile, tile), tile)
        pltpu.make_async_copy(weight_ref.at[0, 0:tile], held_ref.at[n], held_sem.at[n]).wait()
        grads = dot(rows_ref[...], held_ref[n], LANES)
        gate = gate_ref[own ^ k]
        for unit in range(units):
            chosen = chosen_ref[k, unit]
            by_token = dot(chosen, kept_ref[k, unit, :, span], ROWS)
            grad = grads[unit * tokens : (unit + 1) * tokens] + gate * adapted_ref[unit, :, span]
            partial = jnp.sum(by_token * grad, axis=1, keepdims=True)
            own_rows = slice(unit * tokens, (unit + 1) * tokens)
            results_ref[own_rows] += jnp.where(lane == k, partial, F32(0.0))
            share = jnp.concatenate([shares_ref[k, own_rows]] * (tile // 128), axis=1)
            shared = dot(chosen, (share * grad).astype(BF16), PLAIN)
            hidden_ref[k, unit, :, span] = shared.astype(BF16)

    for unit in range(units):
        dots_ref[unit] = results_ref[unit * tokens : (unit + 1) * tokens].T[:8]
    writes = []
    for unit in range(units):
        source = place_ref[2 + unit]
        for value, target in (
            (dots_ref.at[unit], dots_out.at[source >> 1]),
            (hidden_ref.at[0, unit], hidden_out.at[source]),
            (hidden_ref.at[1, unit], other_out.at[slot + unit]),
        ):
            writes.append(pltpu.make_async_copy(value, target, write_sem.at[len(writes)]))
            writes[-1].start()
    mark_ref[...] = jnp.zeros(mark_ref.shape, F32)
    for copy in writes:
        copy.wait()


def expert_call(place, gate, weight, other_weight, stored, other_stored, first, got, buffers, hidden, other, dots, mark, slot):
    devices, cap, width_hidden = stored.shape
    layout = [(len(as_end), len(as_mid)) for as_end, as_mid in buffers]
    pieces = [piece for pair in buffers for side in pair for piece in side]
    width = pieces[0].shape[1]
    tokens = got.shape[2]
    units = len(buffers)
    any_spec = pl.BlockSpec(memory_space=pl.ANY)
    smem = pl.BlockSpec(memory_space=pltpu.SMEM)
    operands = [place, gate, weight, other_weight, stored, other_stored, first, got, *pieces]
    in_specs = [smem] * 2 + [any_spec] * 4 + whole(2) + [any_spec] * len(pieces)
    if mark is not None:
        operands.append(mark)
        in_specs.append(any_spec)
    aliases, sizes = {}, []
    for number, value in enumerate((hidden, other, dots)):
        if isinstance(value, int):
            sizes.append(value)
        else:
            sizes.append(value.shape[0])
            aliases[len(operands)] = number
            operands.append(value)
            in_specs.append(any_spec)
    loads = max(sum(counts[role] for counts in layout) for role in range(2))
    return pl.pallas_call(
        functools.partial(expert_kernel, layout=layout, slot=slot),
        in_specs=in_specs,
        out_specs=[any_spec, any_spec, any_spec, pl.BlockSpec(memory_space=pltpu.VMEM)],
        out_shape=[
            jax.ShapeDtypeStruct((sizes[0], cap, width_hidden), BF16),
            jax.ShapeDtypeStruct((sizes[1], cap, width_hidden), BF16),
            jax.ShapeDtypeStruct((sizes[2], 8, tokens), F32),
            jax.ShapeDtypeStruct((8, 128), F32),
        ],
        scratch_shapes=[
            pltpu.VMEM((units * tokens, width), BF16),
            pltpu.VMEM((2 * width_hidden // TILE, TILE, width), BF16),
            pltpu.VMEM((2, units, cap, width_hidden), BF16),
            pltpu.VMEM((2, units, cap, width_hidden), BF16),
            pltpu.VMEM((units, 8, tokens), F32),
            pltpu.VMEM((units, tokens, width_hidden), F32),
            pltpu.VMEM((2, units, cap, tokens), BF16),
            pltpu.VMEM((2, units * tokens, 128), F32),
            pltpu.VMEM((units * tokens, 128), F32),
            pltpu.SemaphoreType.DMA((loads,)),
            pltpu.SemaphoreType.DMA((2 * width_hidden // TILE,)),
            pltpu.SemaphoreType.DMA((2 * units,)),
            pltpu.SemaphoreType.DMA((3 * units,)),
        ],
        input_output_aliases=aliases,
        compiler_params=params(BIG_LIMIT),
        cost_estimate=SMALL,
    )(*operands)


def place_kernel(own_ref, *refs, masks):
    hidden_ref, sem = refs[-2:]
    copies = []
    for moved_ref, turns in zip(refs, masks):
        for k, mask in enumerate(turns):
            source = own_ref[0] ^ 1 ^ (mask << 1)
            copies.append(pltpu.make_async_copy(moved_ref.at[k], hidden_ref.at[source], sem.at[len(copies)]))
    for copy in copies:
        copy.start()
    for copy in copies:
        copy.wait()


def place_call(own1, moved, hidden, masks):
    any_spec = pl.BlockSpec(memory_space=pl.ANY)
    return pl.pallas_call(
        functools.partial(place_kernel, masks=masks),
        in_specs=[pl.BlockSpec(memory_space=pltpu.SMEM)] + whole(len(moved)) + [any_spec],
        out_specs=any_spec,
        out_shape=jax.ShapeDtypeStruct(hidden.shape, hidden.dtype),
        input_output_aliases={1 + len(moved): 0},
        scratch_shapes=[pltpu.SemaphoreType.DMA((sum(len(turns) for turns in masks),))],
        compiler_params=params(),
        cost_estimate=SMALL,
    )(own1, *moved, hidden)


def finish_kernel(own_ref, dots_ref, routes_ref, moved_ref, _, __, routing_ref, hidden_ref, sem, *, mask):
    own = own_ref[0]
    copy = pltpu.make_async_copy(moved_ref.at[0], hidden_ref.at[own ^ 1 ^ (mask << 1)], sem)
    copy.start()
    routes = routes_ref[...]
    total = jnp.zeros(routes.shape, F32)
    for chip in range(dots_ref.shape[0]):
        for row in range(2):
            expert = 2 * chip + ((own & 1) ^ row)
            total = total + jnp.where(routes == expert, dots_ref[chip, row : row + 1, :], F32(0.0))
    routing_ref[...] = total
    copy.wait()


def permutes():
    number = lambda z, x, c: (z * 2 + x) * 2 + c
    places = [(z, x, c) for z in range(4) for x in range(2) for c in range(2)]
    end = lambda z: z in (0, 3)
    return dict(
        near=[(number(z, x, c), number(z ^ 1, x, c)) for z, x, c in places],
        mid=[(number(z, x, c), number(3 - z, x, c)) for z, x, c in places if not end(z)],
        out=[(number(z, x, c), number(z ^ 1, x, c)) for z, x, c in places if not end(z)],
        side=[(number(z, x, c), number(z, 1 - x, c)) for z, x, c in places],
        end_side=[(number(z, x, c), number(z, 1 - x, c)) for z, x, c in places if end(z)],
    )


def xor_pairs(mask):
    return [(i, i ^ mask) for i in range(16)]


def send(value, pairs):
    return lax.ppermute(value, "ex", pairs)


def then(value, *earlier):
    return lax.optimization_barrier((value, *earlier))[0]


def small_body(
    gradient_mantissas,
    gradient_exponents,
    routes,
    routing_weight,
    stored_hidden_rows,
    frozen_down_weight,
    adapter_first_factor,
    adapter_second_factor,
    expert_adapter_gate,
):
    tokens, width = gradient_mantissas.shape
    stored = stored_hidden_rows[0]
    devices, cap, hidden = stored.shape
    rank = adapter_second_factor.shape[0]
    first = adapter_first_factor.T
    routes_t, weights_t = routes.T, routing_weight.T
    own = lax.axis_index("ex").astype(jnp.int32)
    own1 = own.reshape(1)
    z = own >> 2
    is_end = ((z == 0) | (z == 3)).astype(jnp.int32)

    smem = pl.BlockSpec(memory_space=pltpu.SMEM)
    vmem = pl.BlockSpec(memory_space=pltpu.VMEM)
    any_spec = pl.BlockSpec(memory_space=pl.ANY)
    to = permutes()
    pick = lambda as_end, as_mid: jnp.where(is_end == 1, as_end, as_mid)

    smem = pl.BlockSpec(memory_space=pltpu.SMEM)
    vmem = pl.BlockSpec(memory_space=pltpu.VMEM)
    any_spec = pl.BlockSpec(memory_space=pl.ANY)
    to = permutes()
    pick = lambda as_end, as_mid: jnp.where(is_end == 1, as_end, as_mid)

    other_weight = send(frozen_down_weight, xor_pairs(1))
    other_stored = send(stored, xor_pairs(1))
    rows = pl.pallas_call(
        scale_kernel,
        in_specs=whole(2),
        out_specs=vmem,
        out_shape=jax.ShapeDtypeStruct((tokens, width), BF16),
        compiler_params=params(),
        cost_estimate=SMALL,
    )(gradient_mantissas, gradient_exponents.T)
    masks = (0, 2, 1, 4, 3, 6, 5, 7)
    final = len(masks) - 1
    half = tokens // 2
    hidden_part, other_part, dots, mark, begin = devices, 5, devices // 2, None, 0

    def experts(count, buffers, *earlier):
        nonlocal hidden_part, other_part, dots, mark, begin
        turns = masks[begin : begin + count]
        place = jnp.stack([own, is_end] + [own ^ (mask << 1) for mask in turns])
        hidden_part, other_part, dots, mark = expert_call(
            then(place, *earlier),
            expert_adapter_gate,
            frozen_down_weight,
            other_weight,
            stored,
            other_stored,
            first,
            got,
            buffers,
            hidden_part,
            other_part,
            dots,
            mark,
            begin if begin < 5 else 0,
        )
        begin += count
        return mark

    near, side, mid = send(rows, to["near"]), send(rows, to["side"]), send(rows, to["mid"])
    packed = pl.pallas_call(
        pack_kernel,
        in_specs=[smem] + whole(6) + [smem],
        out_specs=vmem,
        out_shape=jax.ShapeDtypeStruct((devices, 2 * rank + devices, tokens), BF16),
        compiler_params=params(),
        cost_estimate=SMALL,
    )(
        then(own1, other_stored),
        rows,
        adapter_second_factor,
        routes_t,
        weights_t,
        stored,
        first,
        expert_adapter_gate,
    )
    got = lax.all_to_all(packed, "ex", split_axis=0, concat_axis=0, tiled=True)
    near, side, mid, _, _ = lax.optimization_barrier((near, side, mid, got, other_weight))
    near2 = send(pick(side, mid), to["near"])
    side2 = send(pick(near, mid), to["side"])
    mid2 = send(near, to["mid"])
    partial = pl.pallas_call(
        low_rank_kernel,
        in_specs=[smem] + whole(3) + [smem] + whole(3),
        out_specs=vmem,
        out_shape=jax.ShapeDtypeStruct((devices, 80, 128), F32),
        scratch_shapes=[pltpu.VMEM((rank, width), F32), pltpu.VMEM((devices, 16, 128), F32)],
        compiler_params=params(),
        cost_estimate=SMALL,
    )(then(own1, near, side, mid), got, stored, first, expert_adapter_gate, routes_t, weights_t, rows)
    lanes = [[2 * chip + core for chip in range(devices // 2)] for core in range(2)]
    among_lane = lambda value: lax.all_to_all(
        value, "ex", split_axis=0, concat_axis=0, axis_index_groups=lanes, tiled=True
    )
    pair = (partial[: devices // 2] + send(partial[devices // 2 :], xor_pairs(1))).astype(BF16)
    parts = among_lane(pair)
    found = experts(1, [([rows], [rows])], pair, near, side, mid)
    near2, mid2, side2, parts, _ = lax.optimization_barrier((near2, mid2, side2, parts, found))
    near3 = send(mid2, to["out"])
    side3 = send(pick(near2, mid2), to["side"])
    summed = jnp.sum(parts.astype(F32), axis=0).astype(BF16)
    summed = among_lane(jnp.broadcast_to(summed[None], (devices // 2, 80, 128)))
    found = experts(4, [([near], [near]), ([side], [side]), ([near2], [mid2]), ([side2], [near2])], near2, side2, mid2)
    near3, side3, summed, _ = lax.optimization_barrier((near3, side3, summed, found))
    last = [send(near3[:half], to["end_side"]), send(side3[half:], to["out"])]
    moved, other_part = [send(then(other_part, near3, side3), xor_pairs(1))], 2
    found = experts(2, [([near3], [mid]), ([side3], [side3])], near3, side3, moved[0])
    summed = then(summed, found)
    summed = jnp.concatenate([summed, send(summed, xor_pairs(1))], axis=0)
    moved.append(send(other_part, xor_pairs(1)))
    other_part = 1
    found = experts(1, [(last, [side2])], *last)
    last_moved = send(other_part, xor_pairs(1))
    second_grad, first_grad, gate_grad = pl.pallas_call(
        unpack_kernel,
        in_specs=[smem] + whole(1),
        out_specs=whole(3),
        out_shape=[
            jax.ShapeDtypeStruct((rank, width), F32),
            jax.ShapeDtypeStruct((rank, hidden), F32),
            jax.ShapeDtypeStruct((8, 128), F32),
        ],
        scratch_shapes=[pltpu.VMEM((devices, 16, 128), F32)],
        compiler_params=params(),
        cost_estimate=SMALL,
    )(then(own1, found), summed)
    hidden_part = place_call(own1, moved, hidden_part, (masks[:5], masks[5:final]))
    moved = last_moved
    returned = among_lane(dots)
    routing_t, hidden_gradient = pl.pallas_call(
        functools.partial(finish_kernel, mask=masks[-1]),
        in_specs=[smem] + whole(3) + [any_spec, any_spec],
        out_specs=[vmem, any_spec],
        out_shape=[
            jax.ShapeDtypeStruct(routes_t.shape, F32),
            jax.ShapeDtypeStruct((devices, cap, hidden), BF16),
        ],
        input_output_aliases={4: 1},
        scratch_shapes=[pltpu.SemaphoreType.DMA],
        compiler_params=params(),
        cost_estimate=SMALL,
    )(own1, returned, routes_t, moved, hidden_part, mark)
    return (
        hidden_gradient[None],
        routing_t.T,
        first_grad.T,
        second_grad,
        gate_grad[0, :devices],
    )


def block_scale(gradient_exponents):
    scaling = jnp.zeros(gradient_exponents.shape, jnp.float32)
    for exponent in range(-2, 3):
        scaling = scaling + jnp.where(
            gradient_exponents == exponent, jnp.float32(2.0**exponent), jnp.float32(0.0)
        )
    return scaling


def expand_grad(gradient_mantissas, gradient_exponents):
    blocks = gradient_exponents.shape[1]
    scaling = block_scale(gradient_exponents)
    widened = (
        gradient_mantissas.astype(jnp.float32).reshape(gradient_mantissas.shape[0], blocks, -1)
        * scaling[:, :, None]
    )
    return widened.reshape(gradient_mantissas.shape).astype(jnp.bfloat16)


def slot_table(route_block, experts, capacity):
    flat_routes = route_block.reshape(-1)
    onehot = (flat_routes[:, None] == jnp.arange(experts, dtype=jnp.int32)[None, :]).astype(
        jnp.int32
    )
    running = jnp.cumsum(onehot, axis=0) - 1
    slot_index = jnp.sum(running * onehot, axis=1)
    return flat_routes * capacity + slot_index


def reduced_projection(current_row_block, adapter_second_factor):
    return lax.dot_general(
        current_row_block,
        adapter_second_factor,
        (((1,), (1,)), ((), ())),
        preferred_element_type=jnp.float32,
    ).astype(jnp.bfloat16)


def per_expert_terms(
    current_row_block,
    routing_share,
    reduced_input,
    stored_rows,
    expert_down_matrix,
    adapter_first_factor,
    expert_gate_value,
):
    contract_dimensions = (((1,), (1,)), ((), ()))
    base_term = lax.dot_general(
        current_row_block,
        expert_down_matrix,
        contract_dimensions,
        preferred_element_type=jnp.float32,
    )
    adapter_side_term = lax.dot_general(
        reduced_input, adapter_first_factor, contract_dimensions, preferred_element_type=jnp.float32
    )
    combined = base_term + expert_gate_value * adapter_side_term
    share_col = routing_share.astype(jnp.float32)[:, None]
    hidden_gradient = (share_col * combined).astype(jnp.bfloat16)
    weight_grad = jnp.sum(stored_rows.astype(jnp.float32) * combined, axis=1)
    low_float = reduced_input.astype(jnp.float32)
    rows_dims = (((0,), (0,)), ((), ()))
    pushed = (expert_gate_value * share_col * low_float).astype(jnp.bfloat16)
    a_grad = lax.dot_general(stored_rows, pushed, rows_dims, preferred_element_type=jnp.float32)
    reduced_rank_rows = jnp.dot(
        stored_rows, adapter_first_factor, preferred_element_type=jnp.float32
    )
    pulled = (expert_gate_value * share_col * reduced_rank_rows).astype(jnp.bfloat16)
    b_grad = lax.dot_general(
        pulled, current_row_block, rows_dims, preferred_element_type=jnp.float32
    )
    gate_term = jnp.sum(
        routing_share.astype(jnp.float32) * jnp.sum(reduced_rank_rows * low_float, axis=1)
    )
    return (hidden_gradient, weight_grad, a_grad, b_grad, gate_term)


def body(
    gradient_mantissas,
    gradient_exponents,
    routes,
    routing_weight,
    stored_hidden_rows,
    frozen_down_weight,
    adapter_first_factor,
    adapter_second_factor,
    expert_adapter_gate,
):
    experts = expert_adapter_gate.shape[0]
    sources = stored_hidden_rows.shape[1]
    capacity = stored_hidden_rows.shape[2]
    hidden_width = stored_hidden_rows.shape[3]
    tok_count, top_count = routes.shape
    slots_all = experts * capacity
    grad_out = expand_grad(gradient_mantissas, gradient_exponents)
    dest = slot_table(routes, experts, capacity)
    token_ids = jnp.arange(tok_count * top_count, dtype=jnp.int32) // top_count
    token_of = jnp.zeros((slots_all,), jnp.int32).at[dest].set(token_ids)
    share_send = (
        jnp.zeros((slots_all,), jnp.bfloat16)
        .at[dest]
        .set(routing_weight.reshape(-1))
        .reshape(experts, capacity)
    )
    row_send = grad_out[token_of].reshape(experts, capacity, -1)
    received_rows = sources * capacity
    token_low = reduced_projection(grad_out, adapter_second_factor)
    low_send = token_low[token_of].reshape(experts, capacity, -1)
    row_recv, share_recv, low_recv = (
        lax.all_to_all(row_send, "ex", split_axis=0, concat_axis=0, tiled=True),
        lax.all_to_all(share_send, "ex", split_axis=0, concat_axis=0, tiled=True),
        lax.all_to_all(low_send, "ex", split_axis=0, concat_axis=0, tiled=True),
    )
    current_row_block = row_recv.reshape(received_rows, -1)
    reduced_input = low_recv.reshape(received_rows, -1)
    routing_share = share_recv.reshape(received_rows)
    stored_rows = stored_hidden_rows.reshape(received_rows, hidden_width)
    expert_down_matrix = frozen_down_weight[0]
    own_index = lax.axis_index("ex")
    expert_gate_value = lax.dynamic_index_in_dim(expert_adapter_gate, own_index, 0, keepdims=False)
    hidden_gradient, weight_grad, a_grad, b_grad, gate_term = per_expert_terms(
        current_row_block,
        routing_share,
        reduced_input,
        stored_rows,
        expert_down_matrix,
        adapter_first_factor,
        expert_gate_value,
    )
    returned = lax.all_to_all(
        weight_grad.reshape(sources, capacity), "ex", split_axis=0, concat_axis=0, tiled=True
    )
    routing_gradient = returned.reshape(-1)[dest].reshape(tok_count, top_count)
    own_gate = (jnp.arange(experts, dtype=jnp.int32) == own_index).astype(jnp.float32) * gate_term
    a_total, b_total, gate_total = lax.psum((a_grad, b_grad, own_gate), "ex")
    hidden_out = hidden_gradient.reshape(1, sources, capacity, hidden_width)
    return (hidden_out, routing_gradient, a_total, b_total, gate_total)


def solution(mesh):
    return jax.shard_map(
        small_body if mesh.shape["ex"] == 16 else body,
        mesh=mesh,
        in_specs=(
            P(("groups", "ex"), None),
            P(("groups", "ex"), None),
            P(("groups", "ex"), None),
            P(("groups", "ex"), None),
            P(("groups", "ex"), None, None, None),
            P("ex", None, None),
            P(),
            P(),
            P(),
        ),
        out_specs=(
            P(("groups", "ex"), None, None, None),
            P(("groups", "ex"), None),
            P("groups", None),
            P("groups", None),
            P("groups"),
        ),
        check_vma=False,
    )
```

```python
import functools

import jax
import jax.numpy as jnp
from jax import lax
from jax.experimental import pallas as pl
from jax.experimental.pallas import tpu as pltpu
from jax.sharding import PartitionSpec as P

F32, BF16 = jnp.float32, jnp.bfloat16
VMEM_LIMIT = 16 * 1024 * 1024
BIG_LIMIT = 50 * 1024 * 1024
TILE, AHEAD = 384, 2
ROWS = (((0,), (0,)), ((), ()))
LANES = (((1,), (1,)), ((), ()))
PLAIN = (((1,), (0,)), ((), ()))


def dot(a, b, dims):
    return lax.dot_general(a, b, dims, preferred_element_type=F32)


SMALL = pl.CostEstimate(flops=1000000, bytes_accessed=10000, transcendentals=0)

LARGE = pl.CostEstimate(flops=30000000000, bytes_accessed=10000, transcendentals=0)


def params(limit=VMEM_LIMIT):
    return pltpu.CompilerParams(vmem_limit_bytes=limit)


def whole(count):
    return [pl.BlockSpec(memory_space=pltpu.VMEM)] * count


def scale_kernel(mantissa_ref, exponent_ref, rows_ref):
    exponents = exponent_ref[...]
    scale = jnp.zeros(exponents.shape, F32)
    for power in range(-2, 3):
        scale = scale + jnp.where(exponents == power, F32(2.0**power), F32(0.0))
    columns = scale.T
    width = mantissa_ref.shape[1] // exponents.shape[0]
    for block in range(exponents.shape[0]):
        lanes = slice(block * width, (block + 1) * width)
        rows_ref[:, lanes] = (mantissa_ref[:, lanes].astype(F32) * columns[:, block : block + 1]).astype(BF16)


def share_table(routes, weights, experts):
    expert = lax.broadcasted_iota(jnp.int32, (experts, routes.shape[1]), 0)
    table = jnp.zeros(expert.shape, F32)
    for k in range(routes.shape[0]):
        table = table + jnp.where(routes[k : k + 1] == expert, weights[k : k + 1], F32(0.0))
    return table


def pack_kernel(
    own_ref, rows_ref, second_ref, routes_ref, weights_ref, stored_ref, first_ref, gate_ref, out_ref
):
    devices, cap = stored_ref.shape[0], stored_ref.shape[1]
    rank = second_ref.shape[0]
    gate = gate_ref[own_ref[0]]
    reduced = dot(second_ref[...], rows_ref[...], LANES).astype(BF16)
    table = share_table(routes_ref[...], weights_ref[...].astype(F32), devices).astype(BF16)
    first = first_ref[...]
    pad = jnp.zeros((rank, out_ref.shape[2] - cap), BF16)
    for peer in range(devices):
        out_ref[peer, 0:rank, :] = reduced
        pulled = (gate * dot(first, stored_ref[peer], LANES)).astype(BF16)
        out_ref[peer, rank : 2 * rank, :] = jnp.concatenate([pulled, pad], axis=1)
        out_ref[peer, 2 * rank :, :] = table


def slot_of(table):
    tokens = table.shape[1]
    earlier = lax.broadcasted_iota(jnp.int32, (tokens, tokens), 0) < lax.broadcasted_iota(
        jnp.int32, (tokens, tokens), 1
    )
    taken = jnp.where(table > 0, F32(1.0), F32(0.0)).astype(BF16)
    count = dot(taken, jnp.where(earlier, F32(1.0), F32(0.0)).astype(BF16), PLAIN)
    return jnp.where(table > 0, count, F32(-1.0)).astype(jnp.int32)


def take_row(table, row):
    rows = lax.broadcasted_iota(jnp.int32, table.shape, 0)
    return jnp.sum(jnp.where(rows == row, table, F32(0.0)), axis=0, keepdims=True)


def chunk_of(j, own, devices):
    half = devices // 2
    return 2 * j + (own & 1) if j < half else 2 * (j - half) + ((own & 1) ^ 1)


def low_rank_kernel(
    own_ref,
    got_ref,
    stored_ref,
    first_ref,
    gate_ref,
    routes_ref,
    weights_ref,
    rows_ref,
    out_ref,
    wide_ref,
    narrow_ref,
):
    devices, cap = stored_ref.shape[0], stored_ref.shape[1]
    own = own_ref[0]
    rank = first_ref.shape[0]
    tokens = got_ref.shape[2]
    gate = gate_ref[own]
    shares = jnp.concatenate(
        [take_row(got_ref[s, 2 * rank :, :].astype(F32), own) for s in range(devices)], axis=0
    )
    slots = slot_of(shares)
    place = lax.broadcasted_iota(jnp.int32, (tokens, tokens), 0)
    total = jnp.zeros((rank, stored_ref.shape[2]), F32)
    for s in range(devices):
        chosen = jnp.where(place == slots[s : s + 1], F32(1.0), F32(0.0)).astype(BF16)
        pushed = (got_ref[s, 0:rank, :].astype(F32) * shares[s : s + 1]).astype(BF16)
        by_slot = dot(pushed, chosen[:cap], LANES).astype(BF16)
        total = total + dot(by_slot, stored_ref[s], PLAIN)
    gate_term = jnp.sum(total * first_ref[...].astype(F32))
    total = gate * total
    narrow_ref[...] = jnp.zeros(narrow_ref.shape, F32)
    for i in range(2 * (total.shape[1] // 128)):
        narrow_ref[i] = total[(i % 2) * 16 : (i % 2) * 16 + 16, (i // 2) * 128 : (i // 2) * 128 + 128]
    lane = lax.broadcasted_iota(jnp.int32, (16, 128), 1)
    row = lax.broadcasted_iota(jnp.int32, (16, 128), 0)
    coarse_gate = jnp.full((16, 128), gate_term, F32).astype(BF16).astype(F32)
    parts = jnp.where(row == 0, coarse_gate, gate_term - coarse_gate)
    narrow_ref[devices - 1] = jnp.where((lane == own) & (row < 2), parts, F32(0.0))

    table = share_table(routes_ref[...], weights_ref[...].astype(F32), devices)
    mine = slot_of(table)
    pulled = jnp.zeros((rank, tokens), F32)
    for e in range(devices):
        weighted = jnp.where(place == mine[e : e + 1], table[e : e + 1], F32(0.0)).astype(BF16)
        pulled = pulled + dot(got_ref[e, rank : 2 * rank, :], weighted, PLAIN)
    coarse = pulled.astype(BF16)
    fine = (pulled - coarse.astype(F32)).astype(BF16)
    both = jnp.concatenate([coarse, fine], axis=0)
    result = dot(both, rows_ref[...], PLAIN)
    wide_ref[...] = result[:rank] + result[rank:]
    columns = wide_ref.shape[1] // devices
    for j in range(devices):
        chunk = chunk_of(j, own, devices)
        for b in range(columns // 128):
            lanes = pl.ds(pl.multiple_of(chunk * columns + b * 128, 128), 128)
            out_ref[j, b * rank : (b + 1) * rank, :] = wide_ref[:, lanes]
        out_ref[j, 64:80, :] = narrow_ref[chunk]


def unpack_kernel(own_ref, got_ref, second_ref, first_ref, gate_ref, narrow_ref):
    devices = got_ref.shape[0]
    own = own_ref[0]
    rank = second_ref.shape[0]
    columns = second_ref.shape[1] // devices
    for j in range(devices):
        chunk = chunk_of(j, own, devices)
        for b in range(columns // 128):
            lanes = pl.ds(pl.multiple_of(chunk * columns + b * 128, 128), 128)
            second_ref[:, lanes] = got_ref[j, b * rank : (b + 1) * rank, :].astype(F32)
        narrow_ref[chunk] = got_ref[j, 64:80, :].astype(F32)
    for i in range(2 * (first_ref.shape[1] // 128)):
        first_ref[(i % 2) * 16 : (i % 2) * 16 + 16, (i // 2) * 128 : (i // 2) * 128 + 128] = narrow_ref[i]
    gates = narrow_ref[devices - 1]
    gate_ref[...] = jnp.broadcast_to(gates[0:1] + gates[1:2], gate_ref.shape)


def expert_kernel(
    place_ref,
    gate_ref,
    weight_ref,
    other_weight_ref,
    stored_ref,
    other_stored_ref,
    first_ref,
    got_ref,
    *rest,
    layout,
    slot,
):
    hidden_out, other_out, dots_out, mark_ref, rows_ref, held_ref, kept_ref, hidden_ref, dots_ref = rest[-17:-8]
    adapted_ref, chosen_ref, shares_ref, results_ref, load_sem, held_sem, kept_sem, write_sem = rest[-8:]
    tile = held_ref.shape[1]
    tiles = weight_ref.shape[1] // tile
    own, is_end = place_ref[0], place_ref[1]
    cap = stored_ref.shape[1]
    rank = first_ref.shape[0]
    units = len(layout)
    tokens = rows_ref.shape[0] // units
    choices, taken = ([], []), 0
    for unit, counts in enumerate(layout):
        for role, count in enumerate(counts):
            begin = unit * tokens
            for k in range(count):
                piece = rest[taken]
                target = rows_ref.at[begin : begin + piece.shape[0]]
                choices[role].append(pltpu.make_async_copy(piece, target, load_sem.at[len(choices[role])]))
                begin += piece.shape[0]
                taken += 1
    for flag, copies in ((1, choices[0]), (0, choices[1])):

        @pl.when(is_end == flag)
        def _():
            for copy in copies:
                copy.start()

    kept = []
    for k, stored in enumerate((stored_ref, other_stored_ref)):
        for unit in range(units):
            kept.append(
                pltpu.make_async_copy(
                    stored.at[place_ref[2 + unit]], kept_ref.at[k, unit], kept_sem.at[k * units + unit]
                )
            )
            kept[-1].start()

    def load(n):
        begin = pl.multiple_of(n % tiles * tile, tile)
        at = lambda weight: pltpu.make_async_copy(weight.at[0, pl.ds(begin, tile)], held_ref.at[n], held_sem.at[n])

        @pl.when(n < tiles)
        def _():
            at(weight_ref).start()

        @pl.when(n >= tiles)
        def _():
            at(other_weight_ref).start()

    for n in range(AHEAD):
        load(jnp.int32(n))

    place = lax.broadcasted_iota(jnp.int32, (cap, tokens), 0)
    for unit in range(units):
        source = place_ref[2 + unit]
        table = got_ref[source, 2 * rank :, :].astype(F32)
        shares = jnp.concatenate(
            [take_row(table, own), take_row(table, own ^ 1), jnp.zeros((6, tokens), F32)], axis=0
        )
        slots = slot_of(shares)
        columns = shares.T
        adapted_ref[unit] = dot(got_ref[source, 0:rank, :], first_ref[...], ROWS)
        for k in range(2):
            chosen_ref[k, unit] = jnp.where(place == slots[k : k + 1], F32(1.0), F32(0.0)).astype(BF16)
            shares_ref[k, unit * tokens : (unit + 1) * tokens] = jnp.broadcast_to(columns[:, k : k + 1], (tokens, 128))
    results_ref[...] = jnp.zeros(results_ref.shape, F32)
    for copy in kept:
        copy.wait()
    for flag, copies in ((1, choices[0]), (0, choices[1])):

        @pl.when(is_end == flag)
        def _():
            for copy in copies:
                copy.wait()

    lane = lax.broadcasted_iota(jnp.int32, (tokens, 128), 1)

    @pl.loop(0, 2 * tiles)
    def _(n):
        @pl.when(n + AHEAD < 2 * tiles)
        def _():
            load(n + AHEAD)

        k = n // tiles
        span = pl.ds(pl.multiple_of(n % tiles * tile, tile), tile)
        pltpu.make_async_copy(weight_ref.at[0, 0:tile], held_ref.at[n], held_sem.at[n]).wait()
        grads = dot(rows_ref[...], held_ref[n], LANES)
        gate = gate_ref[own ^ k]
        for unit in range(units):
            chosen = chosen_ref[k, unit]
            by_token = dot(chosen, kept_ref[k, unit, :, span], ROWS)
            grad = grads[unit * tokens : (unit + 1) * tokens] + gate * adapted_ref[unit, :, span]
            partial = jnp.sum(by_token * grad, axis=1, keepdims=True)
            own_rows = slice(unit * tokens, (unit + 1) * tokens)
            results_ref[own_rows] += jnp.where(lane == k, partial, F32(0.0))
            share = jnp.concatenate([shares_ref[k, own_rows]] * (tile // 128), axis=1)
            shared = dot(chosen, (share * grad).astype(BF16), PLAIN)
            hidden_ref[k, unit, :, span] = shared.astype(BF16)

    for unit in range(units):
        dots_ref[unit] = results_ref[unit * tokens : (unit + 1) * tokens].T[:8]
    writes = []
    for unit in range(units):
        source = place_ref[2 + unit]
        for value, target in (
            (dots_ref.at[unit], dots_out.at[source >> 1]),
            (hidden_ref.at[0, unit], hidden_out.at[source]),
            (hidden_ref.at[1, unit], other_out.at[slot + unit]),
        ):
            writes.append(pltpu.make_async_copy(value, target, write_sem.at[len(writes)]))
            writes[-1].start()
    mark_ref[...] = jnp.zeros(mark_ref.shape, F32)
    for copy in writes:
        copy.wait()


def expert_call(place, gate, weight, other_weight, stored, other_stored, first, got, buffers, hidden, other, dots, mark, slot):
    devices, cap, width_hidden = stored.shape
    layout = [(len(as_end), len(as_mid)) for as_end, as_mid in buffers]
    pieces = [piece for pair in buffers for side in pair for piece in side]
    width = pieces[0].shape[1]
    tokens = got.shape[2]
    units = len(buffers)
    any_spec = pl.BlockSpec(memory_space=pl.ANY)
    smem = pl.BlockSpec(memory_space=pltpu.SMEM)
    operands = [place, gate, weight, other_weight, stored, other_stored, first, got, *pieces]
    in_specs = [smem] * 2 + [any_spec] * 4 + whole(2) + [any_spec] * len(pieces)
    if mark is not None:
        operands.append(mark)
        in_specs.append(any_spec)
    aliases, sizes = {}, []
    for number, value in enumerate((hidden, other, dots)):
        if isinstance(value, int):
            sizes.append(value)
        else:
            sizes.append(value.shape[0])
            aliases[len(operands)] = number
            operands.append(value)
            in_specs.append(any_spec)
    loads = max(sum(counts[role] for counts in layout) for role in range(2))
    return pl.pallas_call(
        functools.partial(expert_kernel, layout=layout, slot=slot),
        in_specs=in_specs,
        out_specs=[any_spec, any_spec, any_spec, pl.BlockSpec(memory_space=pltpu.VMEM)],
        out_shape=[
            jax.ShapeDtypeStruct((sizes[0], cap, width_hidden), BF16),
            jax.ShapeDtypeStruct((sizes[1], cap, width_hidden), BF16),
            jax.ShapeDtypeStruct((sizes[2], 8, tokens), F32),
            jax.ShapeDtypeStruct((8, 128), F32),
        ],
        scratch_shapes=[
            pltpu.VMEM((units * tokens, width), BF16),
            pltpu.VMEM((2 * width_hidden // TILE, TILE, width), BF16),
            pltpu.VMEM((2, units, cap, width_hidden), BF16),
            pltpu.VMEM((2, units, cap, width_hidden), BF16),
            pltpu.VMEM((units, 8, tokens), F32),
            pltpu.VMEM((units, tokens, width_hidden), F32),
            pltpu.VMEM((2, units, cap, tokens), BF16),
            pltpu.VMEM((2, units * tokens, 128), F32),
            pltpu.VMEM((units * tokens, 128), F32),
            pltpu.SemaphoreType.DMA((loads,)),
            pltpu.SemaphoreType.DMA((2 * width_hidden // TILE,)),
            pltpu.SemaphoreType.DMA((2 * units,)),
            pltpu.SemaphoreType.DMA((3 * units,)),
        ],
        input_output_aliases=aliases,
        compiler_params=params(BIG_LIMIT),
        cost_estimate=SMALL,
    )(*operands)


def place_kernel(own_ref, *refs, masks):
    hidden_ref, sem = refs[-2:]
    copies = []
    for moved_ref, turns in zip(refs, masks):
        for k, mask in enumerate(turns):
            source = own_ref[0] ^ 1 ^ (mask << 1)
            copies.append(pltpu.make_async_copy(moved_ref.at[k], hidden_ref.at[source], sem.at[len(copies)]))
    for copy in copies:
        copy.start()
    for copy in copies:
        copy.wait()


def place_call(own1, moved, hidden, masks):
    any_spec = pl.BlockSpec(memory_space=pl.ANY)
    return pl.pallas_call(
        functools.partial(place_kernel, masks=masks),
        in_specs=[pl.BlockSpec(memory_space=pltpu.SMEM)] + whole(len(moved)) + [any_spec],
        out_specs=any_spec,
        out_shape=jax.ShapeDtypeStruct(hidden.shape, hidden.dtype),
        input_output_aliases={1 + len(moved): 0},
        scratch_shapes=[pltpu.SemaphoreType.DMA((sum(len(turns) for turns in masks),))],
        compiler_params=params(),
        cost_estimate=SMALL,
    )(own1, *moved, hidden)


def finish_kernel(own_ref, dots_ref, routes_ref, moved_ref, _, __, routing_ref, hidden_ref, sem, *, mask):
    own = own_ref[0]
    copy = pltpu.make_async_copy(moved_ref.at[0], hidden_ref.at[own ^ 1 ^ (mask << 1)], sem)
    copy.start()
    routes = routes_ref[...]
    total = jnp.zeros(routes.shape, F32)
    for chip in range(dots_ref.shape[0]):
        for row in range(2):
            expert = 2 * chip + ((own & 1) ^ row)
            total = total + jnp.where(routes == expert, dots_ref[chip, row : row + 1, :], F32(0.0))
    routing_ref[...] = total
    copy.wait()


def permutes():
    number = lambda z, x, c: (z * 2 + x) * 2 + c
    places = [(z, x, c) for z in range(4) for x in range(2) for c in range(2)]
    end = lambda z: z in (0, 3)
    return dict(
        near=[(number(z, x, c), number(z ^ 1, x, c)) for z, x, c in places],
        mid=[(number(z, x, c), number(3 - z, x, c)) for z, x, c in places if not end(z)],
        out=[(number(z, x, c), number(z ^ 1, x, c)) for z, x, c in places if not end(z)],
        side=[(number(z, x, c), number(z, 1 - x, c)) for z, x, c in places],
        end_side=[(number(z, x, c), number(z, 1 - x, c)) for z, x, c in places if end(z)],
    )


def xor_pairs(mask):
    return [(i, i ^ mask) for i in range(16)]


def send(value, pairs):
    return lax.ppermute(value, "ex", pairs)


def then(value, *earlier):
    return lax.optimization_barrier((value, *earlier))[0]


def small_body(
    gradient_mantissas,
    gradient_exponents,
    routes,
    routing_weight,
    stored_hidden_rows,
    frozen_down_weight,
    adapter_first_factor,
    adapter_second_factor,
    expert_adapter_gate,
):
    tokens, width = gradient_mantissas.shape
    stored = stored_hidden_rows[0]
    devices, cap, hidden = stored.shape
    rank = adapter_second_factor.shape[0]
    first = adapter_first_factor.T
    routes_t, weights_t = routes.T, routing_weight.T
    own = lax.axis_index("ex").astype(jnp.int32)
    own1 = own.reshape(1)
    z = own >> 2
    is_end = ((z == 0) | (z == 3)).astype(jnp.int32)

    smem = pl.BlockSpec(memory_space=pltpu.SMEM)
    vmem = pl.BlockSpec(memory_space=pltpu.VMEM)
    any_spec = pl.BlockSpec(memory_space=pl.ANY)
    to = permutes()
    pick = lambda as_end, as_mid: jnp.where(is_end == 1, as_end, as_mid)

    smem = pl.BlockSpec(memory_space=pltpu.SMEM)
    vmem = pl.BlockSpec(memory_space=pltpu.VMEM)
    any_spec = pl.BlockSpec(memory_space=pl.ANY)
    to = permutes()
    pick = lambda as_end, as_mid: jnp.where(is_end == 1, as_end, as_mid)

    other_weight = send(frozen_down_weight, xor_pairs(1))
    other_stored = send(stored, xor_pairs(1))
    rows = pl.pallas_call(
        scale_kernel,
        in_specs=whole(2),
        out_specs=vmem,
        out_shape=jax.ShapeDtypeStruct((tokens, width), BF16),
        compiler_params=params(),
        cost_estimate=SMALL,
    )(gradient_mantissas, gradient_exponents.T)
    masks = (0, 2, 1, 4, 3, 6, 5, 7)
    final = len(masks) - 1
    half = tokens // 2
    hidden_part, other_part, dots, mark, begin = devices, 5, devices // 2, None, 0

    def experts(count, buffers, *earlier):
        nonlocal hidden_part, other_part, dots, mark, begin
        turns = masks[begin : begin + count]
        place = jnp.stack([own, is_end] + [own ^ (mask << 1) for mask in turns])
        hidden_part, other_part, dots, mark = expert_call(
            then(place, *earlier),
            expert_adapter_gate,
            frozen_down_weight,
            other_weight,
            stored,
            other_stored,
            first,
            got,
            buffers,
            hidden_part,
            other_part,
            dots,
            mark,
            begin if begin < 5 else 0,
        )
        begin += count
        return mark

    near, side, mid = send(rows, to["near"]), send(rows, to["side"]), send(rows, to["mid"])
    packed = pl.pallas_call(
        pack_kernel,
        in_specs=[smem] + whole(6) + [smem],
        out_specs=vmem,
        out_shape=jax.ShapeDtypeStruct((devices, 2 * rank + devices, tokens), BF16),
        compiler_params=params(),
        cost_estimate=SMALL,
    )(
        then(own1, other_stored),
        rows,
        adapter_second_factor,
        routes_t,
        weights_t,
        stored,
        first,
        expert_adapter_gate,
    )
    got = lax.all_to_all(packed, "ex", split_axis=0, concat_axis=0, tiled=True)
    near, side, mid, _, _ = lax.optimization_barrier((near, side, mid, got, other_weight))
    near2 = send(pick(side, mid), to["near"])
    side2 = send(pick(near, mid), to["side"])
    mid2 = send(near, to["mid"])
    partial = pl.pallas_call(
        low_rank_kernel,
        in_specs=[smem] + whole(3) + [smem] + whole(3),
        out_specs=vmem,
        out_shape=jax.ShapeDtypeStruct((devices, 80, 128), F32),
        scratch_shapes=[pltpu.VMEM((rank, width), F32), pltpu.VMEM((devices, 16, 128), F32)],
        compiler_params=params(),
        cost_estimate=SMALL,
    )(then(own1, near, side, mid), got, stored, first, expert_adapter_gate, routes_t, weights_t, rows)
    lanes = [[2 * chip + core for chip in range(devices // 2)] for core in range(2)]
    among_lane = lambda value: lax.all_to_all(
        value, "ex", split_axis=0, concat_axis=0, axis_index_groups=lanes, tiled=True
    )
    pair = (partial[: devices // 2] + send(partial[devices // 2 :], xor_pairs(1))).astype(BF16)
    parts = among_lane(pair)
    found = experts(1, [([rows], [rows])], pair, near, side, mid)
    near2, mid2, side2, parts, _ = lax.optimization_barrier((near2, mid2, side2, parts, found))
    near3 = send(mid2, to["out"])
    side3 = send(pick(near2, mid2), to["side"])
    summed = jnp.sum(parts.astype(F32), axis=0).astype(BF16)
    summed = among_lane(jnp.broadcast_to(summed[None], (devices // 2, 80, 128)))
    found = experts(4, [([near], [near]), ([side], [side]), ([near2], [mid2]), ([side2], [near2])], near2, side2, mid2)
    near3, side3, summed, _ = lax.optimization_barrier((near3, side3, summed, found))
    last = [send(near3[:half], to["end_side"]), send(side3[half:], to["out"])]
    moved, other_part = [send(then(other_part, near3, side3), xor_pairs(1))], 2
    found = experts(2, [([near3], [mid]), ([side3], [side3])], near3, side3, moved[0])
    summed = then(summed, found)
    summed = jnp.concatenate([summed, send(summed, xor_pairs(1))], axis=0)
    moved.append(send(other_part, xor_pairs(1)))
    other_part = 1
    found = experts(1, [(last, [side2])], *last)
    last_moved = send(other_part, xor_pairs(1))
    second_grad, first_grad, gate_grad = pl.pallas_call(
        unpack_kernel,
        in_specs=[smem] + whole(1),
        out_specs=whole(3),
        out_shape=[
            jax.ShapeDtypeStruct((rank, width), F32),
            jax.ShapeDtypeStruct((rank, hidden), F32),
            jax.ShapeDtypeStruct((8, 128), F32),
        ],
        scratch_shapes=[pltpu.VMEM((devices, 16, 128), F32)],
        compiler_params=params(),
        cost_estimate=SMALL,
    )(then(own1, found), summed)
    hidden_part = place_call(own1, moved, hidden_part, (masks[:5], masks[5:final]))
    moved = last_moved
    returned = among_lane(dots)
    routing_t, hidden_gradient = pl.pallas_call(
        functools.partial(finish_kernel, mask=masks[-1]),
        in_specs=[smem] + whole(3) + [any_spec, any_spec],
        out_specs=[vmem, any_spec],
        out_shape=[
            jax.ShapeDtypeStruct(routes_t.shape, F32),
            jax.ShapeDtypeStruct((devices, cap, hidden), BF16),
        ],
        input_output_aliases={4: 1},
        scratch_shapes=[pltpu.SemaphoreType.DMA],
        compiler_params=params(),
        cost_estimate=SMALL,
    )(own1, returned, routes_t, moved, hidden_part, mark)
    return (
        hidden_gradient[None],
        routing_t.T,
        first_grad.T,
        second_grad,
        gate_grad[0, :devices],
    )


def block_scale(gradient_exponents):
    scaling = jnp.zeros(gradient_exponents.shape, jnp.float32)
    for exponent in range(-2, 3):
        scaling = scaling + jnp.where(
            gradient_exponents == exponent, jnp.float32(2.0**exponent), jnp.float32(0.0)
        )
    return scaling


def expand_grad(gradient_mantissas, gradient_exponents):
    blocks = gradient_exponents.shape[1]
    scaling = block_scale(gradient_exponents)
    widened = (
        gradient_mantissas.astype(jnp.float32).reshape(gradient_mantissas.shape[0], blocks, -1)
        * scaling[:, :, None]
    )
    return widened.reshape(gradient_mantissas.shape).astype(jnp.bfloat16)


def slot_table(route_block, experts, capacity):
    flat_routes = route_block.reshape(-1)
    onehot = (flat_routes[:, None] == jnp.arange(experts, dtype=jnp.int32)[None, :]).astype(
        jnp.int32
    )
    running = jnp.cumsum(onehot, axis=0) - 1
    slot_index = jnp.sum(running * onehot, axis=1)
    return flat_routes * capacity + slot_index


def reduced_projection(current_row_block, adapter_second_factor):
    return lax.dot_general(
        current_row_block,
        adapter_second_factor,
        (((1,), (1,)), ((), ())),
        preferred_element_type=jnp.float32,
    ).astype(jnp.bfloat16)


def per_expert_terms(
    current_row_block,
    routing_share,
    reduced_input,
    stored_rows,
    expert_down_matrix,
    adapter_first_factor,
    expert_gate_value,
):
    contract_dimensions = (((1,), (1,)), ((), ()))
    base_term = lax.dot_general(
        current_row_block,
        expert_down_matrix,
        contract_dimensions,
        preferred_element_type=jnp.float32,
    )
    adapter_side_term = lax.dot_general(
        reduced_input, adapter_first_factor, contract_dimensions, preferred_element_type=jnp.float32
    )
    combined = base_term + expert_gate_value * adapter_side_term
    share_col = routing_share.astype(jnp.float32)[:, None]
    hidden_gradient = (share_col * combined).astype(jnp.bfloat16)
    weight_grad = jnp.sum(stored_rows.astype(jnp.float32) * combined, axis=1)
    low_float = reduced_input.astype(jnp.float32)
    rows_dims = (((0,), (0,)), ((), ()))
    pushed = (expert_gate_value * share_col * low_float).astype(jnp.bfloat16)
    a_grad = lax.dot_general(stored_rows, pushed, rows_dims, preferred_element_type=jnp.float32)
    reduced_rank_rows = jnp.dot(
        stored_rows, adapter_first_factor, preferred_element_type=jnp.float32
    )
    pulled = (expert_gate_value * share_col * reduced_rank_rows).astype(jnp.bfloat16)
    b_grad = lax.dot_general(
        pulled, current_row_block, rows_dims, preferred_element_type=jnp.float32
    )
    gate_term = jnp.sum(
        routing_share.astype(jnp.float32) * jnp.sum(reduced_rank_rows * low_float, axis=1)
    )
    return (hidden_gradient, weight_grad, a_grad, b_grad, gate_term)


def body(
    gradient_mantissas,
    gradient_exponents,
    routes,
    routing_weight,
    stored_hidden_rows,
    frozen_down_weight,
    adapter_first_factor,
    adapter_second_factor,
    expert_adapter_gate,
):
    experts = expert_adapter_gate.shape[0]
    sources = stored_hidden_rows.shape[1]
    capacity = stored_hidden_rows.shape[2]
    hidden_width = stored_hidden_rows.shape[3]
    tok_count, top_count = routes.shape
    slots_all = experts * capacity
    grad_out = expand_grad(gradient_mantissas, gradient_exponents)
    dest = slot_table(routes, experts, capacity)
    token_ids = jnp.arange(tok_count * top_count, dtype=jnp.int32) // top_count
    token_of = jnp.zeros((slots_all,), jnp.int32).at[dest].set(token_ids)
    share_send = (
        jnp.zeros((slots_all,), jnp.bfloat16)
        .at[dest]
        .set(routing_weight.reshape(-1))
        .reshape(experts, capacity)
    )
    row_send = grad_out[token_of].reshape(experts, capacity, -1)
    received_rows = sources * capacity
    token_low = reduced_projection(grad_out, adapter_second_factor)
    low_send = token_low[token_of].reshape(experts, capacity, -1)
    row_recv, share_recv, low_recv = (
        lax.all_to_all(row_send, "ex", split_axis=0, concat_axis=0, tiled=True),
        lax.all_to_all(share_send, "ex", split_axis=0, concat_axis=0, tiled=True),
        lax.all_to_all(low_send, "ex", split_axis=0, concat_axis=0, tiled=True),
    )
    current_row_block = row_recv.reshape(received_rows, -1)
    reduced_input = low_recv.reshape(received_rows, -1)
    routing_share = share_recv.reshape(received_rows)
    stored_rows = stored_hidden_rows.reshape(received_rows, hidden_width)
    expert_down_matrix = frozen_down_weight[0]
    own_index = lax.axis_index("ex")
    expert_gate_value = lax.dynamic_index_in_dim(expert_adapter_gate, own_index, 0, keepdims=False)
    hidden_gradient, weight_grad, a_grad, b_grad, gate_term = per_expert_terms(
        current_row_block,
        routing_share,
        reduced_input,
        stored_rows,
        expert_down_matrix,
        adapter_first_factor,
        expert_gate_value,
    )
    returned = lax.all_to_all(
        weight_grad.reshape(sources, capacity), "ex", split_axis=0, concat_axis=0, tiled=True
    )
    routing_gradient = returned.reshape(-1)[dest].reshape(tok_count, top_count)
    own_gate = (jnp.arange(experts, dtype=jnp.int32) == own_index).astype(jnp.float32) * gate_term
    a_total, b_total, gate_total = lax.psum((a_grad, b_grad, own_gate), "ex")
    hidden_out = hidden_gradient.reshape(1, sources, capacity, hidden_width)
    return (hidden_out, routing_gradient, a_total, b_total, gate_total)


def solution(mesh):
    return jax.shard_map(
        small_body if mesh.shape["ex"] == 16 else body,
        mesh=mesh,
        in_specs=(
            P(("groups", "ex"), None),
            P(("groups", "ex"), None),
            P(("groups", "ex"), None),
            P(("groups", "ex"), None),
            P(("groups", "ex"), None, None, None),
            P("ex", None, None),
            P(),
            P(),
            P(),
        ),
        out_specs=(
            P(("groups", "ex"), None, None, None),
            P(("groups", "ex"), None),
            P("groups", None),
            P("groups", None),
            P("groups"),
        ),
        check_vma=False,
    )
```

```python
import functools

import jax
import jax.numpy as jnp
from jax import lax
from jax.experimental import pallas as pl
from jax.experimental.pallas import tpu as pltpu
from jax.sharding import PartitionSpec as P

F32, BF16 = jnp.float32, jnp.bfloat16
VMEM_LIMIT = 16 * 1024 * 1024
BIG_LIMIT = 48 * 1024 * 1024
TILE, AHEAD = 384, 2
ROWS = (((0,), (0,)), ((), ()))
LANES = (((1,), (1,)), ((), ()))
PLAIN = (((1,), (0,)), ((), ()))


def dot(a, b, dims):
    return lax.dot_general(a, b, dims, preferred_element_type=F32)


SMALL = pl.CostEstimate(flops=1000000, bytes_accessed=10000, transcendentals=0)

LARGE = pl.CostEstimate(flops=30000000000, bytes_accessed=10000, transcendentals=0)


def params(limit=VMEM_LIMIT):
    return pltpu.CompilerParams(vmem_limit_bytes=limit)


def whole(count):
    return [pl.BlockSpec(memory_space=pltpu.VMEM)] * count


def scale_kernel(mantissa_ref, exponent_ref, rows_ref):
    exponents = exponent_ref[...]
    scale = jnp.zeros(exponents.shape, F32)
    for power in range(-2, 3):
        scale = scale + jnp.where(exponents == power, F32(2.0**power), F32(0.0))
    columns = scale.T
    width = mantissa_ref.shape[1] // exponents.shape[0]
    for block in range(exponents.shape[0]):
        lanes = slice(block * width, (block + 1) * width)
        rows_ref[:, lanes] = (mantissa_ref[:, lanes].astype(F32) * columns[:, block : block + 1]).astype(BF16)


def share_table(routes, weights, experts):
    expert = lax.broadcasted_iota(jnp.int32, (experts, routes.shape[1]), 0)
    table = jnp.zeros(expert.shape, F32)
    for k in range(routes.shape[0]):
        table = table + jnp.where(routes[k : k + 1] == expert, weights[k : k + 1], F32(0.0))
    return table


def pack_kernel(
    own_ref, rows_ref, second_ref, routes_ref, weights_ref, stored_ref, first_ref, gate_ref, out_ref
):
    devices, cap = stored_ref.shape[0], stored_ref.shape[1]
    rank = second_ref.shape[0]
    gate = gate_ref[own_ref[0]]
    reduced = dot(second_ref[...], rows_ref[...], LANES).astype(BF16)
    table = share_table(routes_ref[...], weights_ref[...].astype(F32), devices).astype(BF16)
    first = first_ref[...]
    pad = jnp.zeros((rank, out_ref.shape[2] - cap), BF16)
    for peer in range(devices):
        out_ref[peer, 0:rank, :] = reduced
        pulled = (gate * dot(first, stored_ref[peer], LANES)).astype(BF16)
        out_ref[peer, rank : 2 * rank, :] = jnp.concatenate([pulled, pad], axis=1)
        out_ref[peer, 2 * rank :, :] = table


def slot_of(table):
    tokens = table.shape[1]
    earlier = lax.broadcasted_iota(jnp.int32, (tokens, tokens), 0) < lax.broadcasted_iota(
        jnp.int32, (tokens, tokens), 1
    )
    taken = jnp.where(table > 0, F32(1.0), F32(0.0)).astype(BF16)
    count = dot(taken, jnp.where(earlier, F32(1.0), F32(0.0)).astype(BF16), PLAIN)
    return jnp.where(table > 0, count, F32(-1.0)).astype(jnp.int32)


def take_row(table, row):
    rows = lax.broadcasted_iota(jnp.int32, table.shape, 0)
    return jnp.sum(jnp.where(rows == row, table, F32(0.0)), axis=0, keepdims=True)


def chunk_of(j, own, devices):
    half = devices // 2
    return 2 * j + (own & 1) if j < half else 2 * (j - half) + ((own & 1) ^ 1)


def low_rank_kernel(
    own_ref,
    got_ref,
    stored_ref,
    first_ref,
    gate_ref,
    routes_ref,
    weights_ref,
    rows_ref,
    out_ref,
    wide_ref,
    narrow_ref,
):
    devices, cap = stored_ref.shape[0], stored_ref.shape[1]
    own = own_ref[0]
    rank = first_ref.shape[0]
    tokens = got_ref.shape[2]
    gate = gate_ref[own]
    shares = jnp.concatenate(
        [take_row(got_ref[s, 2 * rank :, :].astype(F32), own) for s in range(devices)], axis=0
    )
    slots = slot_of(shares)
    place = lax.broadcasted_iota(jnp.int32, (tokens, tokens), 0)
    total = jnp.zeros((rank, stored_ref.shape[2]), F32)
    for s in range(devices):
        chosen = jnp.where(place == slots[s : s + 1], F32(1.0), F32(0.0)).astype(BF16)
        pushed = (got_ref[s, 0:rank, :].astype(F32) * shares[s : s + 1]).astype(BF16)
        by_slot = dot(pushed, chosen[:cap], LANES).astype(BF16)
        total = total + dot(by_slot, stored_ref[s], PLAIN)
    gate_term = jnp.sum(total * first_ref[...].astype(F32))
    total = gate * total
    narrow_ref[...] = jnp.zeros(narrow_ref.shape, F32)
    for i in range(2 * (total.shape[1] // 128)):
        narrow_ref[i] = total[(i % 2) * 16 : (i % 2) * 16 + 16, (i // 2) * 128 : (i // 2) * 128 + 128]
    lane = lax.broadcasted_iota(jnp.int32, (16, 128), 1)
    row = lax.broadcasted_iota(jnp.int32, (16, 128), 0)
    coarse_gate = jnp.full((16, 128), gate_term, F32).astype(BF16).astype(F32)
    parts = jnp.where(row == 0, coarse_gate, gate_term - coarse_gate)
    narrow_ref[devices - 1] = jnp.where((lane == own) & (row < 2), parts, F32(0.0))

    table = share_table(routes_ref[...], weights_ref[...].astype(F32), devices)
    mine = slot_of(table)
    pulled = jnp.zeros((rank, tokens), F32)
    for e in range(devices):
        weighted = jnp.where(place == mine[e : e + 1], table[e : e + 1], F32(0.0)).astype(BF16)
        pulled = pulled + dot(got_ref[e, rank : 2 * rank, :], weighted, PLAIN)
    coarse = pulled.astype(BF16)
    fine = (pulled - coarse.astype(F32)).astype(BF16)
    both = jnp.concatenate([coarse, fine], axis=0)
    result = dot(both, rows_ref[...], PLAIN)
    wide_ref[...] = result[:rank] + result[rank:]
    columns = wide_ref.shape[1] // devices
    for j in range(devices):
        chunk = chunk_of(j, own, devices)
        for b in range(columns // 128):
            lanes = pl.ds(pl.multiple_of(chunk * columns + b * 128, 128), 128)
            out_ref[j, b * rank : (b + 1) * rank, :] = wide_ref[:, lanes]
        out_ref[j, 64:80, :] = narrow_ref[chunk]


def unpack_kernel(own_ref, got_ref, second_ref, first_ref, gate_ref, narrow_ref):
    devices = got_ref.shape[0]
    own = own_ref[0]
    rank = second_ref.shape[0]
    columns = second_ref.shape[1] // devices
    for j in range(devices):
        chunk = chunk_of(j, own, devices)
        for b in range(columns // 128):
            lanes = pl.ds(pl.multiple_of(chunk * columns + b * 128, 128), 128)
            second_ref[:, lanes] = got_ref[j, b * rank : (b + 1) * rank, :].astype(F32)
        narrow_ref[chunk] = got_ref[j, 64:80, :].astype(F32)
    for i in range(2 * (first_ref.shape[1] // 128)):
        first_ref[(i % 2) * 16 : (i % 2) * 16 + 16, (i // 2) * 128 : (i // 2) * 128 + 128] = narrow_ref[i]
    gates = narrow_ref[devices - 1]
    gate_ref[...] = jnp.broadcast_to(gates[0:1] + gates[1:2], gate_ref.shape)


def expert_kernel(
    place_ref,
    gate_ref,
    weight_ref,
    other_weight_ref,
    stored_ref,
    other_stored_ref,
    first_ref,
    got_ref,
    *rest,
    layout,
    slot,
):
    hidden_out, other_out, dots_out, mark_ref, rows_ref, held_ref, kept_ref, hidden_ref, dots_ref = rest[-17:-8]
    adapted_ref, chosen_ref, shares_ref, results_ref, load_sem, held_sem, kept_sem, write_sem = rest[-8:]
    tile = held_ref.shape[1]
    tiles = weight_ref.shape[1] // tile
    own, is_end = place_ref[0], place_ref[1]
    cap = stored_ref.shape[1]
    rank = first_ref.shape[0]
    units = len(layout)
    tokens = rows_ref.shape[0] // units
    choices, taken = ([], []), 0
    for unit, counts in enumerate(layout):
        for role, count in enumerate(counts):
            begin = unit * tokens
            for k in range(count):
                piece = rest[taken]
                target = rows_ref.at[begin : begin + piece.shape[0]]
                choices[role].append(pltpu.make_async_copy(piece, target, load_sem.at[len(choices[role])]))
                begin += piece.shape[0]
                taken += 1
    for flag, copies in ((1, choices[0]), (0, choices[1])):

        @pl.when(is_end == flag)
        def _():
            for copy in copies:
                copy.start()

    kept = []
    for k, stored in enumerate((stored_ref, other_stored_ref)):
        for unit in range(units):
            kept.append(
                pltpu.make_async_copy(
                    stored.at[place_ref[2 + unit]], kept_ref.at[k, unit], kept_sem.at[k * units + unit]
                )
            )
            kept[-1].start()

    def load(n):
        begin = pl.multiple_of(n % tiles * tile, tile)
        at = lambda weight: pltpu.make_async_copy(weight.at[0, pl.ds(begin, tile)], held_ref.at[n], held_sem.at[n])

        @pl.when(n < tiles)
        def _():
            at(weight_ref).start()

        @pl.when(n >= tiles)
        def _():
            at(other_weight_ref).start()

    for n in range(AHEAD):
        load(jnp.int32(n))

    place = lax.broadcasted_iota(jnp.int32, (cap, tokens), 0)
    for unit in range(units):
        source = place_ref[2 + unit]
        table = got_ref[source, 2 * rank :, :].astype(F32)
        shares = jnp.concatenate(
            [take_row(table, own), take_row(table, own ^ 1), jnp.zeros((6, tokens), F32)], axis=0
        )
        slots = slot_of(shares)
        columns = shares.T
        adapted_ref[unit] = dot(got_ref[source, 0:rank, :], first_ref[...], ROWS)
        for k in range(2):
            chosen_ref[k, unit] = jnp.where(place == slots[k : k + 1], F32(1.0), F32(0.0)).astype(BF16)
            shares_ref[k, unit * tokens : (unit + 1) * tokens] = jnp.broadcast_to(columns[:, k : k + 1], (tokens, 128))
    results_ref[...] = jnp.zeros(results_ref.shape, F32)
    for copy in kept:
        copy.wait()
    for flag, copies in ((1, choices[0]), (0, choices[1])):

        @pl.when(is_end == flag)
        def _():
            for copy in copies:
                copy.wait()

    lane = lax.broadcasted_iota(jnp.int32, (tokens, 128), 1)

    @pl.loop(0, 2 * tiles)
    def _(n):
        @pl.when(n + AHEAD < 2 * tiles)
        def _():
            load(n + AHEAD)

        k = n // tiles
        span = pl.ds(pl.multiple_of(n % tiles * tile, tile), tile)
        pltpu.make_async_copy(weight_ref.at[0, 0:tile], held_ref.at[n], held_sem.at[n]).wait()
        grads = dot(rows_ref[...], held_ref[n], LANES)
        gate = gate_ref[own ^ k]
        for unit in range(units):
            chosen = chosen_ref[k, unit]
            by_token = dot(chosen, kept_ref[k, unit, :, span], ROWS)
            grad = grads[unit * tokens : (unit + 1) * tokens] + gate * adapted_ref[unit, :, span]
            partial = jnp.sum(by_token * grad, axis=1, keepdims=True)
            own_rows = slice(unit * tokens, (unit + 1) * tokens)
            results_ref[own_rows] += jnp.where(lane == k, partial, F32(0.0))
            share = jnp.concatenate([shares_ref[k, own_rows]] * (tile // 128), axis=1)
            shared = dot(chosen, (share * grad).astype(BF16), PLAIN)
            hidden_ref[k, unit, :, span] = shared.astype(BF16)

    for unit in range(units):
        dots_ref[unit] = results_ref[unit * tokens : (unit + 1) * tokens].T[:8]
    writes = []
    for unit in range(units):
        source = place_ref[2 + unit]
        for value, target in (
            (dots_ref.at[unit], dots_out.at[source >> 1]),
            (hidden_ref.at[0, unit], hidden_out.at[source]),
            (hidden_ref.at[1, unit], other_out.at[slot + unit]),
        ):
            writes.append(pltpu.make_async_copy(value, target, write_sem.at[len(writes)]))
            writes[-1].start()
    mark_ref[...] = jnp.zeros(mark_ref.shape, F32)
    for copy in writes:
        copy.wait()


def expert_call(place, gate, weight, other_weight, stored, other_stored, first, got, buffers, hidden, other, dots, mark, slot):
    devices, cap, width_hidden = stored.shape
    layout = [(len(as_end), len(as_mid)) for as_end, as_mid in buffers]
    pieces = [piece for pair in buffers for side in pair for piece in side]
    width = pieces[0].shape[1]
    tokens = got.shape[2]
    units = len(buffers)
    any_spec = pl.BlockSpec(memory_space=pl.ANY)
    smem = pl.BlockSpec(memory_space=pltpu.SMEM)
    operands = [place, gate, weight, other_weight, stored, other_stored, first, got, *pieces]
    in_specs = [smem] * 2 + [any_spec] * 4 + whole(2) + [any_spec] * len(pieces)
    if mark is not None:
        operands.append(mark)
        in_specs.append(any_spec)
    aliases, sizes = {}, []
    for number, value in enumerate((hidden, other, dots)):
        if isinstance(value, int):
            sizes.append(value)
        else:
            sizes.append(value.shape[0])
            aliases[len(operands)] = number
            operands.append(value)
            in_specs.append(any_spec)
    loads = max(sum(counts[role] for counts in layout) for role in range(2))
    return pl.pallas_call(
        functools.partial(expert_kernel, layout=layout, slot=slot),
        in_specs=in_specs,
        out_specs=[any_spec, any_spec, any_spec, pl.BlockSpec(memory_space=pltpu.VMEM)],
        out_shape=[
            jax.ShapeDtypeStruct((sizes[0], cap, width_hidden), BF16),
            jax.ShapeDtypeStruct((sizes[1], cap, width_hidden), BF16),
            jax.ShapeDtypeStruct((sizes[2], 8, tokens), F32),
            jax.ShapeDtypeStruct((8, 128), F32),
        ],
        scratch_shapes=[
            pltpu.VMEM((units * tokens, width), BF16),
            pltpu.VMEM((2 * width_hidden // TILE, TILE, width), BF16),
            pltpu.VMEM((2, units, cap, width_hidden), BF16),
            pltpu.VMEM((2, units, cap, width_hidden), BF16),
            pltpu.VMEM((units, 8, tokens), F32),
            pltpu.VMEM((units, tokens, width_hidden), F32),
            pltpu.VMEM((2, units, cap, tokens), BF16),
            pltpu.VMEM((2, units * tokens, 128), F32),
            pltpu.VMEM((units * tokens, 128), F32),
            pltpu.SemaphoreType.DMA((loads,)),
            pltpu.SemaphoreType.DMA((2 * width_hidden // TILE,)),
            pltpu.SemaphoreType.DMA((2 * units,)),
            pltpu.SemaphoreType.DMA((3 * units,)),
        ],
        input_output_aliases=aliases,
        compiler_params=params(BIG_LIMIT),
        cost_estimate=SMALL,
    )(*operands)


def place_kernel(own_ref, *refs, masks):
    hidden_ref, sem = refs[-2:]
    copies = []
    for moved_ref, turns in zip(refs, masks):
        for k, mask in enumerate(turns):
            source = own_ref[0] ^ 1 ^ (mask << 1)
            copies.append(pltpu.make_async_copy(moved_ref.at[k], hidden_ref.at[source], sem.at[len(copies)]))
    for copy in copies:
        copy.start()
    for copy in copies:
        copy.wait()


def place_call(own1, moved, hidden, masks):
    any_spec = pl.BlockSpec(memory_space=pl.ANY)
    return pl.pallas_call(
        functools.partial(place_kernel, masks=masks),
        in_specs=[pl.BlockSpec(memory_space=pltpu.SMEM)] + whole(len(moved)) + [any_spec],
        out_specs=any_spec,
        out_shape=jax.ShapeDtypeStruct(hidden.shape, hidden.dtype),
        input_output_aliases={1 + len(moved): 0},
        scratch_shapes=[pltpu.SemaphoreType.DMA((sum(len(turns) for turns in masks),))],
        compiler_params=params(),
        cost_estimate=SMALL,
    )(own1, *moved, hidden)


def finish_kernel(own_ref, dots_ref, routes_ref, moved_ref, _, __, routing_ref, hidden_ref, sem, *, mask):
    own = own_ref[0]
    copy = pltpu.make_async_copy(moved_ref.at[0], hidden_ref.at[own ^ 1 ^ (mask << 1)], sem)
    copy.start()
    routes = routes_ref[...]
    total = jnp.zeros(routes.shape, F32)
    for chip in range(dots_ref.shape[0]):
        for row in range(2):
            expert = 2 * chip + ((own & 1) ^ row)
            total = total + jnp.where(routes == expert, dots_ref[chip, row : row + 1, :], F32(0.0))
    routing_ref[...] = total
    copy.wait()


def permutes():
    number = lambda z, x, c: (z * 2 + x) * 2 + c
    places = [(z, x, c) for z in range(4) for x in range(2) for c in range(2)]
    end = lambda z: z in (0, 3)
    return dict(
        near=[(number(z, x, c), number(z ^ 1, x, c)) for z, x, c in places],
        mid=[(number(z, x, c), number(3 - z, x, c)) for z, x, c in places if not end(z)],
        out=[(number(z, x, c), number(z ^ 1, x, c)) for z, x, c in places if not end(z)],
        side=[(number(z, x, c), number(z, 1 - x, c)) for z, x, c in places],
        end_side=[(number(z, x, c), number(z, 1 - x, c)) for z, x, c in places if end(z)],
    )


def xor_pairs(mask):
    return [(i, i ^ mask) for i in range(16)]


def send(value, pairs):
    return lax.ppermute(value, "ex", pairs)


def then(value, *earlier):
    return lax.optimization_barrier((value, *earlier))[0]


def small_body(
    gradient_mantissas,
    gradient_exponents,
    routes,
    routing_weight,
    stored_hidden_rows,
    frozen_down_weight,
    adapter_first_factor,
    adapter_second_factor,
    expert_adapter_gate,
):
    tokens, width = gradient_mantissas.shape
    stored = stored_hidden_rows[0]
    devices, cap, hidden = stored.shape
    rank = adapter_second_factor.shape[0]
    first = adapter_first_factor.T
    routes_t, weights_t = routes.T, routing_weight.T
    own = lax.axis_index("ex").astype(jnp.int32)
    own1 = own.reshape(1)
    z = own >> 2
    is_end = ((z == 0) | (z == 3)).astype(jnp.int32)

    smem = pl.BlockSpec(memory_space=pltpu.SMEM)
    vmem = pl.BlockSpec(memory_space=pltpu.VMEM)
    any_spec = pl.BlockSpec(memory_space=pl.ANY)
    to = permutes()
    pick = lambda as_end, as_mid: jnp.where(is_end == 1, as_end, as_mid)

    smem = pl.BlockSpec(memory_space=pltpu.SMEM)
    vmem = pl.BlockSpec(memory_space=pltpu.VMEM)
    any_spec = pl.BlockSpec(memory_space=pl.ANY)
    to = permutes()
    pick = lambda as_end, as_mid: jnp.where(is_end == 1, as_end, as_mid)

    other_weight = send(frozen_down_weight, xor_pairs(1))
    other_stored = send(stored, xor_pairs(1))
    rows = pl.pallas_call(
        scale_kernel,
        in_specs=whole(2),
        out_specs=vmem,
        out_shape=jax.ShapeDtypeStruct((tokens, width), BF16),
        compiler_params=params(),
        cost_estimate=SMALL,
    )(gradient_mantissas, gradient_exponents.T)
    masks = (0, 2, 1, 4, 3, 6, 5, 7)
    final = len(masks) - 1
    half = tokens // 2
    hidden_part, other_part, dots, mark, begin = devices, 5, devices // 2, None, 0

    def experts(count, buffers, *earlier):
        nonlocal hidden_part, other_part, dots, mark, begin
        turns = masks[begin : begin + count]
        place = jnp.stack([own, is_end] + [own ^ (mask << 1) for mask in turns])
        hidden_part, other_part, dots, mark = expert_call(
            then(place, *earlier),
            expert_adapter_gate,
            frozen_down_weight,
            other_weight,
            stored,
            other_stored,
            first,
            got,
            buffers,
            hidden_part,
            other_part,
            dots,
            mark,
            begin if begin < 5 else 0,
        )
        begin += count
        return mark

    near, side, mid = send(rows, to["near"]), send(rows, to["side"]), send(rows, to["mid"])
    packed = pl.pallas_call(
        pack_kernel,
        in_specs=[smem] + whole(6) + [smem],
        out_specs=vmem,
        out_shape=jax.ShapeDtypeStruct((devices, 2 * rank + devices, tokens), BF16),
        compiler_params=params(),
        cost_estimate=SMALL,
    )(
        then(own1, other_stored),
        rows,
        adapter_second_factor,
        routes_t,
        weights_t,
        stored,
        first,
        expert_adapter_gate,
    )
    got = lax.all_to_all(packed, "ex", split_axis=0, concat_axis=0, tiled=True)
    near, side, mid, _, _ = lax.optimization_barrier((near, side, mid, got, other_weight))
    near2 = send(pick(side, mid), to["near"])
    side2 = send(pick(near, mid), to["side"])
    mid2 = send(near, to["mid"])
    partial = pl.pallas_call(
        low_rank_kernel,
        in_specs=[smem] + whole(3) + [smem] + whole(3),
        out_specs=vmem,
        out_shape=jax.ShapeDtypeStruct((devices, 80, 128), F32),
        scratch_shapes=[pltpu.VMEM((rank, width), F32), pltpu.VMEM((devices, 16, 128), F32)],
        compiler_params=params(),
        cost_estimate=SMALL,
    )(then(own1, near, side, mid), got, stored, first, expert_adapter_gate, routes_t, weights_t, rows)
    lanes = [[2 * chip + core for chip in range(devices // 2)] for core in range(2)]
    among_lane = lambda value: lax.all_to_all(
        value, "ex", split_axis=0, concat_axis=0, axis_index_groups=lanes, tiled=True
    )
    pair = (partial[: devices // 2] + send(partial[devices // 2 :], xor_pairs(1))).astype(BF16)
    parts = among_lane(pair)
    found = experts(1, [([rows], [rows])], pair, near, side, mid)
    near2, mid2, side2, parts, _ = lax.optimization_barrier((near2, mid2, side2, parts, found))
    near3 = send(mid2, to["out"])
    side3 = send(pick(near2, mid2), to["side"])
    summed = jnp.sum(parts.astype(F32), axis=0).astype(BF16)
    summed = among_lane(jnp.broadcast_to(summed[None], (devices // 2, 80, 128)))
    found = experts(4, [([near], [near]), ([side], [side]), ([near2], [mid2]), ([side2], [near2])], near2, side2, mid2)
    near3, side3, summed, _ = lax.optimization_barrier((near3, side3, summed, found))
    last = [send(near3[:half], to["end_side"]), send(side3[half:], to["out"])]
    moved, other_part = [send(then(other_part, near3, side3), xor_pairs(1))], 2
    found = experts(2, [([near3], [mid]), ([side3], [side3])], near3, side3, moved[0])
    summed = then(summed, found)
    summed = jnp.concatenate([summed, send(summed, xor_pairs(1))], axis=0)
    moved.append(send(other_part, xor_pairs(1)))
    other_part = 1
    found = experts(1, [(last, [side2])], *last)
    last_moved = send(other_part, xor_pairs(1))
    second_grad, first_grad, gate_grad = pl.pallas_call(
        unpack_kernel,
        in_specs=[smem] + whole(1),
        out_specs=whole(3),
        out_shape=[
            jax.ShapeDtypeStruct((rank, width), F32),
            jax.ShapeDtypeStruct((rank, hidden), F32),
            jax.ShapeDtypeStruct((8, 128), F32),
        ],
        scratch_shapes=[pltpu.VMEM((devices, 16, 128), F32)],
        compiler_params=params(),
        cost_estimate=SMALL,
    )(then(own1, found), summed)
    hidden_part = place_call(own1, moved, hidden_part, (masks[:5], masks[5:final]))
    moved = last_moved
    returned = among_lane(dots)
    routing_t, hidden_gradient = pl.pallas_call(
        functools.partial(finish_kernel, mask=masks[-1]),
        in_specs=[smem] + whole(3) + [any_spec, any_spec],
        out_specs=[vmem, any_spec],
        out_shape=[
            jax.ShapeDtypeStruct(routes_t.shape, F32),
            jax.ShapeDtypeStruct((devices, cap, hidden), BF16),
        ],
        input_output_aliases={4: 1},
        scratch_shapes=[pltpu.SemaphoreType.DMA],
        compiler_params=params(),
        cost_estimate=SMALL,
    )(own1, returned, routes_t, moved, hidden_part, mark)
    return (
        hidden_gradient[None],
        routing_t.T,
        first_grad.T,
        second_grad,
        gate_grad[0, :devices],
    )


def block_scale(gradient_exponents):
    scaling = jnp.zeros(gradient_exponents.shape, jnp.float32)
    for exponent in range(-2, 3):
        scaling = scaling + jnp.where(
            gradient_exponents == exponent, jnp.float32(2.0**exponent), jnp.float32(0.0)
        )
    return scaling


def expand_grad(gradient_mantissas, gradient_exponents):
    blocks = gradient_exponents.shape[1]
    scaling = block_scale(gradient_exponents)
    widened = (
        gradient_mantissas.astype(jnp.float32).reshape(gradient_mantissas.shape[0], blocks, -1)
        * scaling[:, :, None]
    )
    return widened.reshape(gradient_mantissas.shape).astype(jnp.bfloat16)


def slot_table(route_block, experts, capacity):
    flat_routes = route_block.reshape(-1)
    onehot = (flat_routes[:, None] == jnp.arange(experts, dtype=jnp.int32)[None, :]).astype(
        jnp.int32
    )
    running = jnp.cumsum(onehot, axis=0) - 1
    slot_index = jnp.sum(running * onehot, axis=1)
    return flat_routes * capacity + slot_index


def reduced_projection(current_row_block, adapter_second_factor):
    return lax.dot_general(
        current_row_block,
        adapter_second_factor,
        (((1,), (1,)), ((), ())),
        preferred_element_type=jnp.float32,
    ).astype(jnp.bfloat16)


def per_expert_terms(
    current_row_block,
    routing_share,
    reduced_input,
    stored_rows,
    expert_down_matrix,
    adapter_first_factor,
    expert_gate_value,
):
    contract_dimensions = (((1,), (1,)), ((), ()))
    base_term = lax.dot_general(
        current_row_block,
        expert_down_matrix,
        contract_dimensions,
        preferred_element_type=jnp.float32,
    )
    adapter_side_term = lax.dot_general(
        reduced_input, adapter_first_factor, contract_dimensions, preferred_element_type=jnp.float32
    )
    combined = base_term + expert_gate_value * adapter_side_term
    share_col = routing_share.astype(jnp.float32)[:, None]
    hidden_gradient = (share_col * combined).astype(jnp.bfloat16)
    weight_grad = jnp.sum(stored_rows.astype(jnp.float32) * combined, axis=1)
    low_float = reduced_input.astype(jnp.float32)
    rows_dims = (((0,), (0,)), ((), ()))
    pushed = (expert_gate_value * share_col * low_float).astype(jnp.bfloat16)
    a_grad = lax.dot_general(stored_rows, pushed, rows_dims, preferred_element_type=jnp.float32)
    reduced_rank_rows = jnp.dot(
        stored_rows, adapter_first_factor, preferred_element_type=jnp.float32
    )
    pulled = (expert_gate_value * share_col * reduced_rank_rows).astype(jnp.bfloat16)
    b_grad = lax.dot_general(
        pulled, current_row_block, rows_dims, preferred_element_type=jnp.float32
    )
    gate_term = jnp.sum(
        routing_share.astype(jnp.float32) * jnp.sum(reduced_rank_rows * low_float, axis=1)
    )
    return (hidden_gradient, weight_grad, a_grad, b_grad, gate_term)


def body(
    gradient_mantissas,
    gradient_exponents,
    routes,
    routing_weight,
    stored_hidden_rows,
    frozen_down_weight,
    adapter_first_factor,
    adapter_second_factor,
    expert_adapter_gate,
):
    experts = expert_adapter_gate.shape[0]
    sources = stored_hidden_rows.shape[1]
    capacity = stored_hidden_rows.shape[2]
    hidden_width = stored_hidden_rows.shape[3]
    tok_count, top_count = routes.shape
    slots_all = experts * capacity
    grad_out = expand_grad(gradient_mantissas, gradient_exponents)
    dest = slot_table(routes, experts, capacity)
    token_ids = jnp.arange(tok_count * top_count, dtype=jnp.int32) // top_count
    token_of = jnp.zeros((slots_all,), jnp.int32).at[dest].set(token_ids)
    share_send = (
        jnp.zeros((slots_all,), jnp.bfloat16)
        .at[dest]
        .set(routing_weight.reshape(-1))
        .reshape(experts, capacity)
    )
    row_send = grad_out[token_of].reshape(experts, capacity, -1)
    received_rows = sources * capacity
    token_low = reduced_projection(grad_out, adapter_second_factor)
    low_send = token_low[token_of].reshape(experts, capacity, -1)
    row_recv, share_recv, low_recv = (
        lax.all_to_all(row_send, "ex", split_axis=0, concat_axis=0, tiled=True),
        lax.all_to_all(share_send, "ex", split_axis=0, concat_axis=0, tiled=True),
        lax.all_to_all(low_send, "ex", split_axis=0, concat_axis=0, tiled=True),
    )
    current_row_block = row_recv.reshape(received_rows, -1)
    reduced_input = low_recv.reshape(received_rows, -1)
    routing_share = share_recv.reshape(received_rows)
    stored_rows = stored_hidden_rows.reshape(received_rows, hidden_width)
    expert_down_matrix = frozen_down_weight[0]
    own_index = lax.axis_index("ex")
    expert_gate_value = lax.dynamic_index_in_dim(expert_adapter_gate, own_index, 0, keepdims=False)
    hidden_gradient, weight_grad, a_grad, b_grad, gate_term = per_expert_terms(
        current_row_block,
        routing_share,
        reduced_input,
        stored_rows,
        expert_down_matrix,
        adapter_first_factor,
        expert_gate_value,
    )
    returned = lax.all_to_all(
        weight_grad.reshape(sources, capacity), "ex", split_axis=0, concat_axis=0, tiled=True
    )
    routing_gradient = returned.reshape(-1)[dest].reshape(tok_count, top_count)
    own_gate = (jnp.arange(experts, dtype=jnp.int32) == own_index).astype(jnp.float32) * gate_term
    a_total, b_total, gate_total = lax.psum((a_grad, b_grad, own_gate), "ex")
    hidden_out = hidden_gradient.reshape(1, sources, capacity, hidden_width)
    return (hidden_out, routing_gradient, a_total, b_total, gate_total)


def solution(mesh):
    return jax.shard_map(
        small_body if mesh.shape["ex"] == 16 else body,
        mesh=mesh,
        in_specs=(
            P(("groups", "ex"), None),
            P(("groups", "ex"), None),
            P(("groups", "ex"), None),
            P(("groups", "ex"), None),
            P(("groups", "ex"), None, None, None),
            P("ex", None, None),
            P(),
            P(),
            P(),
        ),
        out_specs=(
            P(("groups", "ex"), None, None, None),
            P(("groups", "ex"), None),
            P("groups", None),
            P("groups", None),
            P("groups"),
        ),
        check_vma=False,
    )
```
